512 devices in a mesh: section: 8 (over z_hi, core), dp: 64 (over y, x, z_lo).
Axes of the slice: x: 4, y: 4, z: 16 (z_hi: 4, z_lo: 4; z = z_hi * 4 + z_lo), core: 2. Of those that a mesh axis runs over, the one named last changes fastest.
Arguments:
- inputs: bfloat16 [2, 4096, 512], P(None, 'dp'), may hold values from -24 to 24
- weights: bfloat16 [8, 1, 512, 512], P('section'), may hold values from -0.125 to 0.125
- cotangent: bfloat16 [2, 4096, 512], P(None, 'dp'), may hold values from -24 to 24
Outputs:
- precond: float32 [8, 1, 512, 512], P('section', None, 'dp')
The draws below stay inside these ranges and needn't reach their ends.
All inputs are finite; a program needn't handle non-finite values.
Results may differ from the reference program's by a relative error of at most 0.01105.
Values may be sent and summed in bfloat16 or wider, within the bound.
A program may use at most 64 MiB of HBM per device.

```python
import math
import jax
import jax.numpy as jnp
from jax import lax

B = 512
LAYERS = 1
MB = 2
SECTIONS = 8
TOKENS = 4096
N_SECTION = 8


def textured(key, fluctuation, spread):
    subkeys = jax.random.split(key, 4)
    columns = jnp.exp(jax.random.uniform(subkeys[0], (B,), minval=math.log(0.3), maxval=math.log(3.0)))
    common = jax.random.truncated_normal(subkeys[1], -2.0, 2.0, (MB, TOKENS, 1))
    direction = jax.random.uniform(subkeys[2], (B,), minval=-1.0, maxval=1.0)
    row_scale = jnp.exp(spread * jax.random.uniform(subkeys[3], (MB, TOKENS, 1)))
    growth = jnp.exp(math.log(3.0) * jnp.arange(TOKENS, dtype=jnp.float32) / TOKENS)[None, :, None]
    values = 0.5 * growth * row_scale * (fluctuation * columns + common * direction)
    return jnp.clip(values, -24.0, 24.0).astype(jnp.bfloat16)


def draw_inputs(key, part):
    key = jax.random.fold_in(key, 17)
    noise_key, shape_key = jax.random.split(key)
    fluctuation = jax.random.truncated_normal(noise_key, -3.0, 3.0, (MB, TOKENS, B))
    return textured(shape_key, fluctuation, math.log(4.0))


def draw_cotangent(key, part):
    key = jax.random.fold_in(key, 29)
    noise_key, shape_key = jax.random.split(key)
    fluctuation = jax.random.truncated_normal(noise_key, -3.0, 3.0, (MB, TOKENS, B))
    return textured(shape_key, fluctuation, math.log(4.0))


def block_scale(stream_key, extent, cuts, low, high):
    gain = 1.0
    for position, shards_of in cuts:
        draws = jax.random.uniform(jax.random.fold_in(jax.random.fold_in(stream_key, 6), position), (shards_of,), jnp.float32, low / len(cuts), high / len(cuts))
        gain = gain * jnp.repeat(jnp.exp(draws), extent[position] // shards_of).reshape((-1,) + (1,) * (len(extent) - 1 - position))
    return gain


def normal_values(rng, extent, scale, limit, cuts=(), held_as=jnp.bfloat16):
    entries = jax.random.normal(rng, extent, jnp.float32) * scale
    if len(cuts) > 0:
        entries = block_scale(rng, extent, cuts, -0.22, 0.18) * entries
    return jnp.clip(entries, min=-limit, max=limit).astype(held_as)


def setup_inputs(seed: int = 0) -> dict:
    streams_of = jax.random.split(jax.random.key(seed), 4)
    inputs = draw_inputs(jax.random.fold_in(streams_of[3], 71), 0)
    weights = normal_values(streams_of[1], (SECTIONS, LAYERS, B, B), (4 * B) ** -0.5, 0.125, ((0, 8),))
    cotangent = draw_cotangent(jax.random.fold_in(streams_of[3], 71), 0)
    return dict(inputs=inputs, weights=weights, cotangent=cotangent)


gelu_coef = 0.7978845608
cubic_coef = 0.044715
damping_level = 0.1
loss_scale = 0.0078125

def gelu_value(values):
    argument = gelu_coef * (values + cubic_coef * values * values * values)
    return 0.5 * values * (1.0 + jnp.tanh(argument))

def gelu_slope(values):
    argument = gelu_coef * (values + cubic_coef * values * values * values)
    tangent = jnp.tanh(argument)
    return 0.5 * (1.0 + tangent) + 0.5 * values * (1.0 - tangent * tangent) * gelu_coef * (1.0 + 3.0 * cubic_coef * values * values)

def chol_solve(lower_factor, right_side):
    middle = lax.linalg.triangular_solve(lower_factor, right_side, left_side=True, lower=True)
    return lax.linalg.triangular_solve(lower_factor, middle, left_side=True, lower=True, transpose_a=True)

def damped_factor(matrix):
    order_size = matrix.shape[-1]
    return jnp.linalg.cholesky(matrix + damping_level * jnp.eye(order_size, dtype=matrix.dtype))

def reference(inputs, weights, cotangent):
    rows_all = MB * TOKENS
    current = inputs.reshape(rows_all, B)
    saved_inputs = []
    saved_preacts = []
    for section_index in range(N_SECTION):
        section_inputs = []
        section_preacts = []
        for level_index in range(LAYERS):
            preact = jnp.dot(current.astype(jnp.float32), weights[section_index, level_index].astype(jnp.float32), preferred_element_type=jnp.float32)
            section_inputs.append(current)
            section_preacts.append(preact)
            current = (current.astype(jnp.float32) + gelu_value(preact)).astype(jnp.bfloat16)
        saved_inputs.append(section_inputs)
        saved_preacts.append(section_preacts)
    upstream = cotangent.reshape(rows_all, B) * loss_scale
    results = [None] * N_SECTION
    for section_index in reversed(range(N_SECTION)):
        per_level = [None] * LAYERS
        for level_index in reversed(range(LAYERS)):
            preact = saved_preacts[section_index][level_index]
            grad_pre = (upstream.astype(jnp.float32) * gelu_slope(preact)).astype(jnp.bfloat16)
            upstream = (upstream.astype(jnp.float32) + jnp.dot(grad_pre.astype(jnp.float32), weights[section_index, level_index].T.astype(jnp.float32), preferred_element_type=jnp.float32)).astype(jnp.bfloat16)
            activations = saved_inputs[section_index][level_index]
            act_factor = jnp.dot(activations.T.astype(jnp.float32), activations.astype(jnp.float32), preferred_element_type=jnp.float32) / rows_all
            grad_factor = jnp.dot(grad_pre.T.astype(jnp.float32), grad_pre.astype(jnp.float32), preferred_element_type=jnp.float32)
            weight_grad = jnp.dot(activations.T.astype(jnp.float32), grad_pre.astype(jnp.float32), preferred_element_type=jnp.float32)
            act_lower = damped_factor(act_factor)
            grad_lower = damped_factor(grad_factor)
            left_solved = chol_solve(act_lower, weight_grad)
            per_level[level_index] = chol_solve(grad_lower, left_solved.T).T
        results[section_index] = jnp.stack(per_level)
    return jnp.stack(results)
```

```python
import functools
import jax
import jax.numpy as jnp
from jax import lax
from jax.experimental import pallas as pl
from jax.experimental.pallas import tpu as pltpu
from jax.sharding import PartitionSpec as P

MESH = pl.DeviceIdType.MESH
HIGHEST = lax.Precision.HIGHEST
F32, BF16 = jnp.float32, jnp.bfloat16
gelu_coef = 0.7978845608
cubic_coef = 0.044715
damping_level = 0.1
loss_scale = 0.0078125

STRIDE = {"y": 16, "x": 4, "z": 1}
PAIRS = [(i, j) for i in range(4) for j in range(i, 4)]
ACT_GROUPS = [(0, 5, "xyz"), (5, 5, "yxz")]
GRAD_GROUPS = [(10, 5, "xyz"), (15, 5, "yxz")]
WEIGHT_GROUPS = [(20, 8, "xyz"), (28, 8, "yxz")]
GATHER_AXES = ["yx", "xy"]


class Place:
    def __init__(self):
        self.section = lax.axis_index("section")
        self.dp = lax.axis_index("dp")
        self.core = lax.rem(self.section, 2)
        self.high = lax.div(self.section, 2)
        self.at = {a: lax.rem(lax.div(self.dp, s), 4) for a, s in STRIDE.items()}

    def along(self, axis, delta):
        there = lax.rem(self.at[axis] + delta, 4)
        return there, (self.section, self.dp + (there - self.at[axis]) * STRIDE[axis])

    def other_high(self, delta):
        return (lax.rem(self.high + delta, 4) * 2 + self.core, self.dp)

    def sibling(self):
        return (self.section + 1 - 2 * self.core, self.dp)


def enter(place):
    barrier = pltpu.get_barrier_semaphore()
    peers = [place.sibling()] + [place.other_high(t) for t in range(1, 4)]
    peers += [place.along(a, t)[1] for a in "yxz" for t in range(1, 4)]
    for peer in peers:
        pl.semaphore_signal(barrier, inc=1, device_id=peer, device_id_type=MESH)
    pl.semaphore_wait(barrier, len(peers))


def remote(src, dst, send, recv, peer):
    return pltpu.make_async_remote_copy(
        src_ref=src, dst_ref=dst, send_sem=send, recv_sem=recv, device_id=peer, device_id_type=MESH
    )


def times(index, size):
    return pl.multiple_of(index * size, size)


class Gather:
    def __init__(self, place, own, full, send, recv):
        self.place, self.own, self.full, self.send, self.recv = place, own, full, send, recv
        self.sent = []

    def rows(self, half, coarse):
        last, first = (self.place.at[a] for a in GATHER_AXES[half])
        if coarse:
            return pl.ds(times(last, 128), 128)
        return pl.ds(pl.multiple_of(last * 128 + first * 32, 32), 32)

    def go(self, index, src, dst, peer):
        copy = remote(src, dst, self.send.at[index], self.recv.at[index], peer)
        copy.start()
        self.sent.append(copy)
        return copy

    def run(self):
        place, full = self.place, self.full
        mine = full.at[place.core]
        pending = [[], []]
        for t in (1, 3, 2):
            for half in range(2):
                part = (self.rows(half, False), pl.ds(half * 256, 256))
                pending[half].append(self.go(
                    6 * half + t - 1, self.own.at[part], mine.at[(t, *part)], place.other_high(4 - t)
                ))
        swaps = [self.go(31, self.own, mine.at[0], place.sibling())]
        for phase in range(2):
            for half in range(2):
                for copy in pending[half]:
                    copy.wait_recv()
                block = mine.at[pl.ds(1, 3), self.rows(half, phase == 1), pl.ds(half * 256, 256)]
                axis = GATHER_AXES[half][1 - phase]
                pending[half] = [
                    self.go(6 * half + (3 if phase == 0 else 12) + d - 1, block, block, place.along(axis, d)[1])
                    for d in (1, 3, 2)
                ]
                if phase == 1:
                    swaps.append(self.go(24 + half, block, block, place.sibling()))
        for number, d in enumerate((1, 3, 2)):
            for half in range(2):
                pending[half][number].wait_recv()
                origin = lax.rem(place.at[GATHER_AXES[half][0]] + 4 - d, 4)
                block = mine.at[pl.ds(1, 3), pl.ds(times(origin, 128), 128), pl.ds(half * 256, 256)]
                swaps.append(self.go(26 + half + 6 + 2 * number, block, block, place.sibling()))
        for copy in swaps:
            copy.wait_recv()

    def close(self):
        for copy in self.sent:
            copy.wait_send()


class Sum:
    def __init__(self, place, group, index, part, full, bufs, send, recv):
        self.place, self.index, self.part, self.full = place, index, part, full
        self.first, self.count, self.axes = group
        self.recv1, self.sum1, self.recv2, self.sum2, self.recv3 = bufs
        self.send, self.recv = send, recv
        self.peers = {a: [place.along(a, d) for d in range(1, 4)] for a in self.axes}

    def copies(self, phase):
        blocks, at = pl.ds(self.first, self.count), self.place.at
        a1, a2, a3 = self.axes
        fine = pl.ds(pl.multiple_of(at[a1] * 32 + at[a2] * 8, 8), 8)
        axis = (a1, a2, a3, a2, a1)[phase]
        made = []
        for d, (there, peer) in enumerate(self.peers[axis]):
            if phase == 0:
                src, dst = self.part.at[blocks, pl.ds(times(there, 32), 32)], self.recv1.at[d, blocks]
            elif phase == 1:
                src, dst = self.sum1.at[blocks, pl.ds(times(there, 8), 8)], self.recv2.at[d, blocks]
            elif phase == 2:
                src, dst = self.sum2.at[blocks], self.recv3.at[d, blocks]
            elif phase == 3:
                src = dst = self.full.at[blocks, fine]
            else:
                src = dst = self.full.at[blocks, pl.ds(times(at[a1], 32), 32)]
            made.append(remote(
                src, dst, self.send.at[self.index, phase, d], self.recv.at[self.index, phase, d], peer
            ))
        return made

    def step(self, phase):
        blocks, at = pl.ds(self.first, self.count), self.place.at
        a1, a2, _ = self.axes
        if phase > 0:
            for copy in self.copies(phase - 1):
                copy.wait_recv()
        if phase == 1:
            mine = self.part[blocks, pl.ds(times(at[a1], 32), 32)]
            self.sum1[blocks] = (mine + self.recv1[0, blocks]) + (self.recv1[1, blocks] + self.recv1[2, blocks])
        elif phase == 2:
            mine = self.sum1[blocks, pl.ds(times(at[a2], 8), 8)]
            self.sum2[blocks] = (mine + self.recv2[0, blocks]) + (self.recv2[1, blocks] + self.recv2[2, blocks])
        elif phase == 3:
            fine = pl.ds(pl.multiple_of(at[a1] * 32 + at[a2] * 8, 8), 8)
            self.full[blocks, fine] = (self.sum2[blocks] + self.recv3[0, blocks]) + (
                self.recv3[1, blocks] + self.recv3[2, blocks]
            )
        if phase < 5:
            for copy in self.copies(phase):
                copy.start()

    def close(self):
        for phase in range(5):
            for copy in self.copies(phase):
                copy.wait_send()


def transposed_dot(left, right):
    return lax.dot_general(left, right, (((0,), (0,)), ((), ())), preferred_element_type=F32)


def thirds(value):
    high = value.astype(BF16)
    rest = value - high.astype(F32)
    middle = rest.astype(BF16)
    return high, middle, (rest - middle.astype(F32)).astype(BF16)


def panel_inverse(panels, lane0):
    sub = lax.broadcasted_iota(jnp.int32, (8, 128), 0)
    lane = lax.broadcasted_iota(jnp.int32, (8, 128), 1)
    pick = [sub == k for k in range(8)]
    for j in range(4):
        first = lane0 + 8 * j
        own = (lane >= first) & (lane < first + 8)
        eye = (lane - first == sub).astype(F32)
        for rows in panels:
            r = rows[j]
            cols = [jnp.broadcast_to(r[0][:, first + k:first + k + 1], (8, 128)) for k in range(8)]
            r = [jnp.where(own, eye, r[0])] + r[1:]
            for k in range(0, 8, 2):
                c0, c1 = cols[k], cols[k + 1]
                p, o, u, w = c0[k:k + 1, :], c1[k:k + 1, :], c0[k + 1:k + 2, :], c1[k + 1:k + 2, :]
                inv = 1.0 / (p * w - o * u)
                c0 = jnp.where(pick[k], -1.0, jnp.where(pick[k + 1], 0.0, c0))
                c1 = jnp.where(pick[k], 0.0, jnp.where(pick[k + 1], -1.0, c1))
                f0 = (c0 * w - c1 * u) * inv
                f1 = (c1 * p - c0 * o) * inv
                both = pick[k] | pick[k + 1]
                for n in range(k + 2, 8):
                    v = cols[n]
                    cols[n] = (jnp.where(both, 0.0, v) - f0 * v[k:k + 1, :]) - f1 * v[k + 1:k + 2, :]
                r = [(jnp.where(both, 0.0, v) - f0 * v[k:k + 1, :]) - f1 * v[k + 1:k + 2, :] for v in r]
            rows[j] = r
            for t in range(1, 4):
                i = (j + t) % 4
                c = rows[i][0]
                acc = [jnp.where(own, 0.0, c)] + rows[i][1:]
                for k in range(8):
                    wide = jnp.broadcast_to(c[:, first + k:first + k + 1], (8, 128))
                    acc = [v - wide * p[k:k + 1, :] for v, p in zip(acc, r)]
                rows[i] = acc
    return panels


def inverses(m, ahead, lefts, rights, beside, many=2):
    row = lax.broadcasted_iota(jnp.int32, (128, 128), 0)
    lane = lax.broadcasted_iota(jnp.int32, (128, 128), 1)
    short = lane[:32]

    def change(b, tile, q, left, right, live):
        lane0 = 32 * q
        mine = (lane >= lane0) & (lane < lane0 + 32) & live
        keep = mine & ((row < lane0) | (row >= lane0 + 32))
        for i in range(4):
            moved = jnp.dot(left[i], right, preferred_element_type=F32)
            for t in range(4):
                value = m[b, tile[i], tile[t]]
                if t == 0:
                    value = jnp.where(keep if i == 0 else mine, 0.0, value)
                m[b, tile[i], tile[t]] = value - moved[:, t * 128:(t + 1) * 128]

    def step(k, carry):
        beside(k)
        tile = [lax.rem(k + t, 4) for t in range(4)]
        before = [lax.rem(k + 3 + t, 4) for t in range(4)]
        waiting = [(before, 3, [lefts[b, i] for i in range(4)], rights[b], k > 0) for b in range(many)]
        old = [[ahead[b, t] for t in range(4)] for b in range(many)]
        for q in range(4):
            lane0 = 32 * q
            rows = pl.ds(lane0, 32)
            panels = panel_inverse([[[v[8 * i:8 * i + 8] for v in o] for i in range(4)] for o in old], lane0)
            following = []
            for b in range(many):
                change(b, *waiting[b])
                new = [jnp.concatenate([panels[b][i][t] for i in range(4)], axis=0) for t in range(4)]
                for t in range(4):
                    m[b, k, tile[t], rows, :] = new[t]
                left = [jnp.where(short < lane0, -old[b][0], jnp.where(short < lane0 + 32, 0.0, old[b][0]))]
                left += [old[b][t] * jnp.where(k + t >= 4, -1.0, 1.0) for t in range(1, 4)]
                rh, rm, rl = thirds(jnp.concatenate(new, axis=1))
                right = jnp.concatenate([rh, rm, rh, rl, rm, rh], axis=0)
                turned = []
                for i in range(4):
                    lh, lm, ll = thirds(left[i])
                    turned.append(jnp.concatenate([lh, lh, lm, lh, lm, ll], axis=0).T)
                waiting[b] = (tile, q, turned, right, True)
                if q < 3:
                    some, block, turn = pl.ds(lane0 + 32, 32), k, turned[0][lane0 + 32:lane0 + 64]
                else:
                    some, block, turn = pl.ds(0, 32), tile[1], turned[1][:32]
                moved = jnp.dot(turn, right, preferred_element_type=F32)
                mine = (short >= lane0) & (short < lane0 + 32)
                nxt = []
                for t in range(4):
                    value = m[b, block, tile[t], some, :]
                    if t == 0:
                        value = jnp.where(mine, 0.0, value)
                    nxt.append(value - moved[:, t * 128:(t + 1) * 128])
                following.append(nxt)
            old = following
        for b in range(many):
            for t in range(4):
                ahead[b, t] = old[b][(t + 1) % 4]
                lefts[b, t] = waiting[b][2][t]
            rights[b] = waiting[b][3]
        return carry

    for b in range(many):
        for t in range(4):
            ahead[b, t] = m[b, 0, t, 0:32, :]
            lefts[b, t] = jnp.zeros((128, 192), BF16)
        rights[b] = jnp.zeros((192, 512), BF16)
    lax.fori_loop(0, 4, step, 0)
    for b in range(many):
        change(b, [3, 0, 1, 2], 3, [lefts[b, i] for i in range(4)], rights[b], True)


def spread(full, first, m, b, scale, column):
    row = lax.broadcasted_iota(jnp.int32, (128, 128), 0)
    lane = lax.broadcasted_iota(jnp.int32, (128, 128), 1)
    down = []
    for i in range(4):
        block = full[first + PAIRS.index((i, i))]
        diagonal = jnp.where(row == lane, block + damping_level, 0.0)
        scale[b, i] = lax.rsqrt(jnp.broadcast_to(jnp.sum(diagonal, axis=0, keepdims=True), (8, 128)))
        down.append(lax.rsqrt(jnp.broadcast_to(jnp.sum(diagonal, axis=1, keepdims=True), (128, 128))))
        if column is not None:
            column[i] = down[i]
    for t, (i, j) in enumerate(PAIRS):
        block = full[first + t]
        if i == j:
            block = jnp.where(row == lane, block + damping_level, block)
        block = (block * down[i]) * scale[b, j, 0:1, :]
        m[b, i, j] = block
        if i != j:
            m[b, j, i] = block.T


def finish(m, full, scale, column, row, out_ref):
    rows = pl.ds(pl.multiple_of(lax.rem(row, 128), 8), 8)
    block = lax.div(row, 128)
    total = None
    for i in range(4):
        left = (m[0, block, i, rows, :] * column[block, rows, :]) * scale[0, i]
        wide = jnp.concatenate([full[20 + i * 4 + j] for j in range(4)], axis=1)
        part = jnp.dot(left, wide, precision=HIGHEST, preferred_element_type=F32)
        total = part if total is None else total + part
    out = None
    for i in range(4):
        wide = jnp.concatenate([m[1, i, j] for j in range(4)], axis=1)
        left = total[:, i * 128:(i + 1) * 128] * scale[1, i]
        part = jnp.dot(left, wide, precision=HIGHEST, preferred_element_type=F32)
        out = part if out is None else out + part
    for j in range(4):
        out_ref[:, j * 128:(j + 1) * 128] = out[:, j * 128:(j + 1) * 128] * scale[1, j]


def kernel(x_hbm, w_hbm, top_hbm, out_ref, weights, kept, slopes, grads, top, part, full,
           recv1, sum1, recv2, sum2, recv3, m, ahead, lefts, rights, scale, column,
           gather_send, gather_recv, sum_send, sum_recv, local):
    place = Place()
    loads = [
        pltpu.make_async_copy(w_hbm, weights.at[place.core, 0], local.at[0]),
        pltpu.make_async_copy(x_hbm, kept.at[0], local.at[1]),
        pltpu.make_async_copy(top_hbm, top, local.at[2]),
    ]
    for load in loads:
        load.start()
    enter(place)
    gather = Gather(place, w_hbm, weights, gather_send, gather_recv)
    gather.run()
    for load in loads:
        load.wait()

    def weight_of(layer):
        return weights.at[lax.rem(layer, 2), lax.rem(lax.div(layer, 2) - place.high + 4, 4)]

    def forward(layer, carry):
        x = kept[layer]
        z = jnp.dot(x, weight_of(layer)[...], preferred_element_type=F32)
        squared = z * z
        tangent = jnp.tanh(gelu_coef * (z + cubic_coef * squared * z))
        slopes[layer] = 0.5 * (1.0 + tangent) + 0.5 * z * (1.0 - tangent * tangent) * gelu_coef * (
            1.0 + 3.0 * cubic_coef * squared
        )
        kept[layer + 1] = (x.astype(F32) + 0.5 * z * (1.0 + tangent)).astype(BF16)
        return carry

    lax.fori_loop(0, 8, forward, 0)

    bufs = (recv1, sum1, recv2, sum2, recv3)
    make = lambda groups, base: [
        Sum(place, g, base + n, part, full, bufs, sum_send, sum_recv) for n, g in enumerate(groups)
    ]
    acts, gradsums, weightsums = make(ACT_GROUPS, 0), make(GRAD_GROUPS, 2), make(WEIGHT_GROUPS, 4)

    def step(groups, phase):
        for group in groups:
            group.step(phase)

    x = kept[place.section]
    for i in range(4):
        product = transposed_dot(x[:, i * 128:(i + 1) * 128], x[:, i * 128:]) * (1.0 / 8192.0)
        for j in range(i, 4):
            part[PAIRS.index((i, j))] = product[:, (j - i) * 128:(j - i + 1) * 128]
    step(acts, 0)

    def backward(number, upstream):
        layer = 7 - number
        grad = (upstream.astype(F32) * slopes[layer]).astype(BF16)
        grads[layer] = grad
        return (
            upstream.astype(F32)
            + lax.dot_general(grad, weight_of(layer)[...], (((1,), (1,)), ((), ())), preferred_element_type=F32)
        ).astype(BF16)

    upstream = (top[...].astype(F32) * loss_scale).astype(BF16)
    lax.fori_loop(0, 8, backward, upstream)
    g = grads[place.section]
    for i in range(4):
        product = transposed_dot(g[:, i * 128:(i + 1) * 128], g[:, i * 128:])
        for j in range(i, 4):
            part[10 + PAIRS.index((i, j))] = product[:, (j - i) * 128:(j - i + 1) * 128]
    step(gradsums, 0)
    step(acts, 1)
    for i in range(4):
        product = transposed_dot(x[:, i * 128:(i + 1) * 128], g)
        for j in range(4):
            part[20 + 4 * i + j] = product[:, j * 128:(j + 1) * 128]
    step(acts, 2)
    step(gradsums, 1)
    step(acts, 3)
    step(gradsums, 2)
    step(weightsums, 0)
    step(acts, 4)
    step(gradsums, 3)
    step(acts, 5)
    spread(full, 0, m, 0, scale, column)
    step(gradsums, 4)
    step(weightsums, 1)
    step(gradsums, 5)
    spread(full, 10, m, 1, scale, None)

    def beside(k):
        for number in range(1, 4):
            pl.when(k == number)(functools.partial(step, weightsums, number + 1))

    inverses(m, ahead, lefts, rights, beside)
    step(weightsums, 5)
    finish(m, full, scale, column, place.dp * 8, out_ref)
    gather.close()
    for group in acts + gradsums + weightsums:
        group.close()


def preconditioned(x, w, top):
    return pl.pallas_call(
        kernel,
        out_shape=jax.ShapeDtypeStruct((8, 512), F32),
        in_specs=[pl.BlockSpec(memory_space=pltpu.HBM)] * 3,
        out_specs=pl.BlockSpec(memory_space=pltpu.VMEM),
        scratch_shapes=[
            pltpu.VMEM((2, 4, 512, 512), BF16),
            pltpu.VMEM((9, 128, 512), BF16),
            pltpu.VMEM((8, 128, 512), F32),
            pltpu.VMEM((8, 128, 512), BF16),
            pltpu.VMEM((128, 512), BF16),
            pltpu.VMEM((36, 128, 128), F32),
            pltpu.VMEM((36, 128, 128), F32),
            pltpu.VMEM((3, 36, 32, 128), F32),
            pltpu.VMEM((36, 32, 128), F32),
            pltpu.VMEM((3, 36, 8, 128), F32),
            pltpu.VMEM((36, 8, 128), F32),
            pltpu.VMEM((3, 36, 8, 128), F32),
            pltpu.VMEM((2, 4, 4, 128, 128), F32),
            pltpu.VMEM((2, 4, 32, 128), F32),
            pltpu.VMEM((2, 4, 128, 192), BF16),
            pltpu.VMEM((2, 192, 512), BF16),
            pltpu.VMEM((2, 4, 8, 128), F32),
            pltpu.VMEM((4, 128, 128), F32),
            pltpu.SemaphoreType.DMA((40,)),
            pltpu.SemaphoreType.DMA((40,)),
            pltpu.SemaphoreType.DMA((6, 5, 3)),
            pltpu.SemaphoreType.DMA((6, 5, 3)),
            pltpu.SemaphoreType.DMA((3,)),
        ],
        compiler_params=pltpu.CompilerParams(
            collective_id=0, has_side_effects=True, vmem_limit_bytes=40 << 20
        ),
    )(x, w, top)


def body(inputs, weights, cotangent):
    rows = preconditioned(inputs.reshape(128, 512), weights[0, 0], cotangent.reshape(128, 512))
    return rows[None, None]


def solution(mesh):
    placed = (P(None, "dp", None), P("section", None, None, None), P(None, "dp", None))
    return jax.shard_map(
        body, mesh=mesh, in_specs=placed, out_specs=P("section", None, "dp", None), check_vma=False
    )
```

```python
import functools
import jax
import jax.numpy as jnp
from jax import lax
from jax.experimental import pallas as pl
from jax.experimental.pallas import tpu as pltpu
from jax.sharding import PartitionSpec as P

MESH = pl.DeviceIdType.MESH
HIGHEST = lax.Precision.HIGHEST
F32, BF16 = jnp.float32, jnp.bfloat16
gelu_coef = 0.7978845608
cubic_coef = 0.044715
damping_level = 0.1
loss_scale = 0.0078125

STRIDE = {"y": 16, "x": 4, "z": 1}
PAIRS = [(i, j) for i in range(4) for j in range(i, 4)]
ACT_GROUPS = [(0, 5, "xyz"), (5, 5, "yxz")]
GRAD_GROUPS = [(10, 5, "xyz"), (15, 5, "yxz")]
WEIGHT_GROUPS = [(20, 8, "xyz"), (28, 8, "yxz")]
GATHER_AXES = ["yx", "xy"]


class Place:
    def __init__(self):
        self.section = lax.axis_index("section")
        self.dp = lax.axis_index("dp")
        self.core = lax.rem(self.section, 2)
        self.high = lax.div(self.section, 2)
        self.at = {a: lax.rem(lax.div(self.dp, s), 4) for a, s in STRIDE.items()}

    def along(self, axis, delta):
        there = lax.rem(self.at[axis] + delta, 4)
        return there, (self.section, self.dp + (there - self.at[axis]) * STRIDE[axis])

    def other_high(self, delta):
        return (lax.rem(self.high + delta, 4) * 2 + self.core, self.dp)

    def sibling(self):
        return (self.section + 1 - 2 * self.core, self.dp)


def enter(place):
    barrier = pltpu.get_barrier_semaphore()
    peers = [place.sibling()] + [place.other_high(t) for t in range(1, 4)]
    peers += [place.along(a, t)[1] for a in "yxz" for t in range(1, 4)]
    for peer in peers:
        pl.semaphore_signal(barrier, inc=1, device_id=peer, device_id_type=MESH)
    pl.semaphore_wait(barrier, len(peers))


def remote(src, dst, send, recv, peer):
    return pltpu.make_async_remote_copy(
        src_ref=src, dst_ref=dst, send_sem=send, recv_sem=recv, device_id=peer, device_id_type=MESH
    )


def times(index, size):
    return pl.multiple_of(index * size, size)


class Gather:
    def __init__(self, place, own, full, send, recv):
        self.place, self.own, self.full, self.send, self.recv = place, own, full, send, recv
        self.sent = []

    def rows(self, half, coarse):
        last, first = (self.place.at[a] for a in GATHER_AXES[half])
        if coarse:
            return pl.ds(times(last, 128), 128)
        return pl.ds(pl.multiple_of(last * 128 + first * 32, 32), 32)

    def go(self, index, src, dst, peer):
        copy = remote(src, dst, self.send.at[index], self.recv.at[index], peer)
        copy.start()
        self.sent.append(copy)
        return copy

    def run(self):
        place, full = self.place, self.full
        mine = full.at[place.core]
        pending = [[], []]
        for t in (1, 3, 2):
            for half in range(2):
                part = (self.rows(half, False), pl.ds(half * 256, 256))
                pending[half].append(self.go(
                    6 * half + t - 1, self.own.at[part], mine.at[(t, *part)], place.other_high(4 - t)
                ))
        swaps = [self.go(31, self.own, mine.at[0], place.sibling())]
        for phase in range(2):
            for half in range(2):
                for copy in pending[half]:
                    copy.wait_recv()
                block = mine.at[pl.ds(1, 3), self.rows(half, phase == 1), pl.ds(half * 256, 256)]
                axis = GATHER_AXES[half][1 - phase]
                pending[half] = [
                    self.go(6 * half + (3 if phase == 0 else 12) + d - 1, block, block, place.along(axis, d)[1])
                    for d in (1, 3, 2)
                ]
                if phase == 1:
                    swaps.append(self.go(24 + half, block, block, place.sibling()))
        for number, d in enumerate((1, 3, 2)):
            for half in range(2):
                pending[half][number].wait_recv()
                origin = lax.rem(place.at[GATHER_AXES[half][0]] + 4 - d, 4)
                block = mine.at[pl.ds(1, 3), pl.ds(times(origin, 128), 128), pl.ds(half * 256, 256)]
                swaps.append(self.go(26 + half + 6 + 2 * number, block, block, place.sibling()))
        for copy in swaps:
            copy.wait_recv()

    def close(self):
        for copy in self.sent:
            copy.wait_send()


class Sum:
    def __init__(self, place, group, index, part, full, bufs, send, recv):
        self.place, self.index, self.part, self.full = place, index, part, full
        self.first, self.count, self.axes = group
        self.recv1, self.sum1, self.recv2, self.sum2, self.recv3 = bufs
        self.send, self.recv = send, recv
        self.peers = {a: [place.along(a, d) for d in range(1, 4)] for a in self.axes}

    def copies(self, phase):
        blocks, at = pl.ds(self.first, self.count), self.place.at
        a1, a2, a3 = self.axes
        fine = pl.ds(pl.multiple_of(at[a1] * 32 + at[a2] * 8, 8), 8)
        axis = (a1, a2, a3, a2, a1)[phase]
        made = []
        for d, (there, peer) in enumerate(self.peers[axis]):
            if phase == 0:
                src, dst = self.part.at[blocks, pl.ds(times(there, 32), 32)], self.recv1.at[d, blocks]
            elif phase == 1:
                src, dst = self.sum1.at[blocks, pl.ds(times(there, 8), 8)], self.recv2.at[d, blocks]
            elif phase == 2:
                src, dst = self.sum2.at[blocks], self.recv3.at[d, blocks]
            elif phase == 3:
                src = dst = self.full.at[blocks, fine]
            else:
                src = dst = self.full.at[blocks, pl.ds(times(at[a1], 32), 32)]
            made.append(remote(
                src, dst, self.send.at[self.index, phase, d], self.recv.at[self.index, phase, d], peer
            ))
        return made

    def step(self, phase):
        blocks, at = pl.ds(self.first, self.count), self.place.at
        a1, a2, _ = self.axes
        if phase > 0:
            for copy in self.copies(phase - 1):
                copy.wait_recv()
        if phase == 1:
            mine = self.part[blocks, pl.ds(times(at[a1], 32), 32)]
            self.sum1[blocks] = (mine + self.recv1[0, blocks]) + (self.recv1[1, blocks] + self.recv1[2, blocks])
        elif phase == 2:
            mine = self.sum1[blocks, pl.ds(times(at[a2], 8), 8)]
            self.sum2[blocks] = (mine + self.recv2[0, blocks]) + (self.recv2[1, blocks] + self.recv2[2, blocks])
        elif phase == 3:
            fine = pl.ds(pl.multiple_of(at[a1] * 32 + at[a2] * 8, 8), 8)
            self.full[blocks, fine] = (self.sum2[blocks] + self.recv3[0, blocks]) + (
                self.recv3[1, blocks] + self.recv3[2, blocks]
            )
        if phase < 5:
            for copy in self.copies(phase):
                copy.start()

    def close(self):
        for phase in range(5):
            for copy in self.copies(phase):
                copy.wait_send()


def transposed_dot(left, right):
    return lax.dot_general(left, right, (((0,), (0,)), ((), ())), preferred_element_type=F32)


def thirds(value):
    high = value.astype(BF16)
    rest = value - high.astype(F32)
    middle = rest.astype(BF16)
    return high, middle, (rest - middle.astype(F32)).astype(BF16)


def panel_inverse(panels, lane0):
    sub = lax.broadcasted_iota(jnp.int32, (8, 128), 0)
    lane = lax.broadcasted_iota(jnp.int32, (8, 128), 1)
    pick = [sub == k for k in range(8)]
    for j in range(4):
        first = lane0 + 8 * j
        own = (lane >= first) & (lane < first + 8)
        eye = (lane - first == sub).astype(F32)
        for rows in panels:
            r = rows[j]
            cols = [jnp.broadcast_to(r[0][:, first + k:first + k + 1], (8, 128)) for k in range(8)]
            r = [jnp.where(own, eye, r[0])] + r[1:]
            for k in range(0, 8, 2):
                c0, c1 = cols[k], cols[k + 1]
                p, o, u, w = c0[k:k + 1, :], c1[k:k + 1, :], c0[k + 1:k + 2, :], c1[k + 1:k + 2, :]
                inv = 1.0 / (p * w - o * u)
                c0 = jnp.where(pick[k], -1.0, jnp.where(pick[k + 1], 0.0, c0))
                c1 = jnp.where(pick[k], 0.0, jnp.where(pick[k + 1], -1.0, c1))
                f0 = (c0 * w - c1 * u) * inv
                f1 = (c1 * p - c0 * o) * inv
                both = pick[k] | pick[k + 1]
                for n in range(k + 2, 8):
                    v = cols[n]
                    cols[n] = (jnp.where(both, 0.0, v) - f0 * v[k:k + 1, :]) - f1 * v[k + 1:k + 2, :]
                r = [(jnp.where(both, 0.0, v) - f0 * v[k:k + 1, :]) - f1 * v[k + 1:k + 2, :] for v in r]
            rows[j] = r
            for t in range(1, 4):
                i = (j + t) % 4
                c = rows[i][0]
                acc = [jnp.where(own, 0.0, c)] + rows[i][1:]
                for k in range(8):
                    wide = jnp.broadcast_to(c[:, first + k:first + k + 1], (8, 128))
                    acc = [v - wide * p[k:k + 1, :] for v, p in zip(acc, r)]
                rows[i] = acc
    return panels


def inverses(m, ahead, lefts, rights, beside, many=2):
    row = lax.broadcasted_iota(jnp.int32, (128, 128), 0)
    lane = lax.broadcasted_iota(jnp.int32, (128, 128), 1)
    short = lane[:32]

    def change(b, tile, q, left, right, live):
        lane0 = 32 * q
        mine = (lane >= lane0) & (lane < lane0 + 32) & live
        keep = mine & ((row < lane0) | (row >= lane0 + 32))
        for i in range(4):
            moved = jnp.dot(left[i], right, preferred_element_type=F32)
            for t in range(4):
                value = m[b, tile[i], tile[t]]
                if t == 0:
                    value = jnp.where(keep if i == 0 else mine, 0.0, value)
                m[b, tile[i], tile[t]] = value - moved[:, t * 128:(t + 1) * 128]

    def step(k, carry):
        beside(k)
        tile = [lax.rem(k + t, 4) for t in range(4)]
        before = [lax.rem(k + 3 + t, 4) for t in range(4)]
        waiting = [(before, 3, [lefts[b, i] for i in range(4)], rights[b], k > 0) for b in range(many)]
        old = [[ahead[b, t] for t in range(4)] for b in range(many)]
        for q in range(4):
            lane0 = 32 * q
            rows = pl.ds(lane0, 32)
            panels = panel_inverse([[[v[8 * i:8 * i + 8] for v in o] for i in range(4)] for o in old], lane0)
            following = []
            for b in range(many):
                change(b, *waiting[b])
                new = [jnp.concatenate([panels[b][i][t] for i in range(4)], axis=0) for t in range(4)]
                for t in range(4):
                    m[b, k, tile[t], rows, :] = new[t]
                left = [jnp.where(short < lane0, -old[b][0], jnp.where(short < lane0 + 32, 0.0, old[b][0]))]
                left += [old[b][t] * jnp.where(k + t >= 4, -1.0, 1.0) for t in range(1, 4)]
                rh, rm, rl = thirds(jnp.concatenate(new, axis=1))
                right = jnp.concatenate([rh, rm, rh, rl, rm, rh], axis=0)
                turned = []
                for i in range(4):
                    lh, lm, ll = thirds(left[i])
                    turned.append(jnp.concatenate([lh, lh, lm, lh, lm, ll], axis=0).T)
                waiting[b] = (tile, q, turned, right, True)
                if q < 3:
                    some, block, turn = pl.ds(lane0 + 32, 32), k, turned[0][lane0 + 32:lane0 + 64]
                else:
                    some, block, turn = pl.ds(0, 32), tile[1], turned[1][:32]
                moved = jnp.dot(turn, right, preferred_element_type=F32)
                mine = (short >= lane0) & (short < lane0 + 32)
                nxt = []
                for t in range(4):
                    value = m[b, block, tile[t], some, :]
                    if t == 0:
                        value = jnp.where(mine, 0.0, value)
                    nxt.append(value - moved[:, t * 128:(t + 1) * 128])
                following.append(nxt)
            old = following
        for b in range(many):
            for t in range(4):
                ahead[b, t] = old[b][(t + 1) % 4]
                lefts[b, t] = waiting[b][2][t]
            rights[b] = waiting[b][3]
        return carry

    for b in range(many):
        for t in range(4):
            ahead[b, t] = m[b, 0, t, 0:32, :]
            lefts[b, t] = jnp.zeros((128, 192), BF16)
        rights[b] = jnp.zeros((192, 512), BF16)
    lax.fori_loop(0, 4, step, 0)
    for b in range(many):
        change(b, [3, 0, 1, 2], 3, [lefts[b, i] for i in range(4)], rights[b], True)


def spread(full, first, m, b, scale, column):
    row = lax.broadcasted_iota(jnp.int32, (128, 128), 0)
    lane = lax.broadcasted_iota(jnp.int32, (128, 128), 1)
    down = []
    for i in range(4):
        block = full[first + PAIRS.index((i, i))]
        diagonal = jnp.where(row == lane, block + damping_level, 0.0)
        scale[b, i] = lax.rsqrt(jnp.broadcast_to(jnp.sum(diagonal, axis=0, keepdims=True), (8, 128)))
        down.append(lax.rsqrt(jnp.broadcast_to(jnp.sum(diagonal, axis=1, keepdims=True), (128, 128))))
        if column is not None:
            column[i] = down[i]
    for t, (i, j) in enumerate(PAIRS):
        block = full[first + t]
        if i == j:
            block = jnp.where(row == lane, block + damping_level, block)
        block = (block * down[i]) * scale[b, j, 0:1, :]
        m[b, i, j] = block
        if i != j:
            m[b, j, i] = block.T


def finish(m, full, scale, column, row, out_ref):
    rows = pl.ds(pl.multiple_of(lax.rem(row, 128), 8), 8)
    block = lax.div(row, 128)
    total = None
    for i in range(4):
        left = (m[0, block, i, rows, :] * column[block, rows, :]) * scale[0, i]
        wide = jnp.concatenate([full[20 + i * 4 + j] for j in range(4)], axis=1)
        part = jnp.dot(left, wide, precision=HIGHEST, preferred_element_type=F32)
        total = part if total is None else total + part
    out = None
    for i in range(4):
        wide = jnp.concatenate([m[1, i, j] for j in range(4)], axis=1)
        left = total[:, i * 128:(i + 1) * 128] * scale[1, i]
        part = jnp.dot(left, wide, precision=HIGHEST, preferred_element_type=F32)
        out = part if out is None else out + part
    for j in range(4):
        out_ref[:, j * 128:(j + 1) * 128] = out[:, j * 128:(j + 1) * 128] * scale[1, j]


def kernel(x_hbm, w_hbm, top_hbm, out_ref, weights, kept, slopes, grads, top, part, full,
           recv1, sum1, recv2, sum2, recv3, m, ahead, lefts, rights, scale, column,
           gather_send, gather_recv, sum_send, sum_recv, local):
    place = Place()
    loads = [
        pltpu.make_async_copy(w_hbm, weights.at[place.core, 0], local.at[0]),
        pltpu.make_async_copy(x_hbm, kept.at[0], local.at[1]),
        pltpu.make_async_copy(top_hbm, top, local.at[2]),
    ]
    for load in loads:
        load.start()
    enter(place)
    gather = Gather(place, w_hbm, weights, gather_send, gather_recv)
    gather.run()
    for load in loads:
        load.wait()

    def weight_of(layer):
        return weights.at[lax.rem(layer, 2), lax.rem(lax.div(layer, 2) - place.high + 4, 4)]

    def forward(layer, carry):
        x = kept[layer]
        z = jnp.dot(x, weight_of(layer)[...], preferred_element_type=F32)
        squared = z * z
        tangent = jnp.tanh(gelu_coef * (z + cubic_coef * squared * z))
        slopes[layer] = 0.5 * (1.0 + tangent) + 0.5 * z * (1.0 - tangent * tangent) * gelu_coef * (
            1.0 + 3.0 * cubic_coef * squared
        )
        kept[layer + 1] = (x.astype(F32) + 0.5 * z * (1.0 + tangent)).astype(BF16)
        return carry

    lax.fori_loop(0, 8, forward, 0)

    bufs = (recv1, sum1, recv2, sum2, recv3)
    make = lambda groups, base: [
        Sum(place, g, base + n, part, full, bufs, sum_send, sum_recv) for n, g in enumerate(groups)
    ]
    acts, gradsums, weightsums = make(ACT_GROUPS, 0), make(GRAD_GROUPS, 2), make(WEIGHT_GROUPS, 4)

    def step(groups, phase):
        for group in groups:
            group.step(phase)

    x = kept[place.section]
    for i in range(4):
        product = transposed_dot(x[:, i * 128:(i + 1) * 128], x[:, i * 128:]) * (1.0 / 8192.0)
        for j in range(i, 4):
            part[PAIRS.index((i, j))] = product[:, (j - i) * 128:(j - i + 1) * 128]
    step(acts, 0)

    def backward(number, upstream):
        layer = 7 - number
        grad = (upstream.astype(F32) * slopes[layer]).astype(BF16)
        grads[layer] = grad
        return (
            upstream.astype(F32)
            + lax.dot_general(grad, weight_of(layer)[...], (((1,), (1,)), ((), ())), preferred_element_type=F32)
        ).astype(BF16)

    upstream = (top[...].astype(F32) * loss_scale).astype(BF16)
    lax.fori_loop(0, 8, backward, upstream)
    g = grads[place.section]
    for i in range(4):
        product = transposed_dot(g[:, i * 128:(i + 1) * 128], g[:, i * 128:])
        for j in range(i, 4):
            part[10 + PAIRS.index((i, j))] = product[:, (j - i) * 128:(j - i + 1) * 128]
    step(gradsums, 0)
    step(acts, 1)
    for i in range(4):
        product = transposed_dot(x[:, i * 128:(i + 1) * 128], g)
        for j in range(4):
            part[20 + 4 * i + j] = product[:, j * 128:(j + 1) * 128]
    step(acts, 2)
    step(gradsums, 1)
    step(weightsums, 0)
    step(acts, 3)
    step(gradsums, 2)
    step(acts, 4)
    step(gradsums, 3)
    step(weightsums, 1)
    step(acts, 5)
    spread(full, 0, m, 0, scale, column)
    step(gradsums, 4)
    step(weightsums, 2)
    step(gradsums, 5)
    spread(full, 10, m, 1, scale, None)

    def beside(k):
        for number in range(1, 3):
            pl.when(k == number)(functools.partial(step, weightsums, number + 2))

    inverses(m, ahead, lefts, rights, beside)
    step(weightsums, 5)
    finish(m, full, scale, column, place.dp * 8, out_ref)
    gather.close()
    for group in acts + gradsums + weightsums:
        group.close()


def preconditioned(x, w, top):
    return pl.pallas_call(
        kernel,
        out_shape=jax.ShapeDtypeStruct((8, 512), F32),
        in_specs=[pl.BlockSpec(memory_space=pltpu.HBM)] * 3,
        out_specs=pl.BlockSpec(memory_space=pltpu.VMEM),
        scratch_shapes=[
            pltpu.VMEM((2, 4, 512, 512), BF16),
            pltpu.VMEM((9, 128, 512), BF16),
            pltpu.VMEM((8, 128, 512), F32),
            pltpu.VMEM((8, 128, 512), BF16),
            pltpu.VMEM((128, 512), BF16),
            pltpu.VMEM((36, 128, 128), F32),
            pltpu.VMEM((36, 128, 128), F32),
            pltpu.VMEM((3, 36, 32, 128), F32),
            pltpu.VMEM((36, 32, 128), F32),
            pltpu.VMEM((3, 36, 8, 128), F32),
            pltpu.VMEM((36, 8, 128), F32),
            pltpu.VMEM((3, 36, 8, 128), F32),
            pltpu.VMEM((2, 4, 4, 128, 128), F32),
            pltpu.VMEM((2, 4, 32, 128), F32),
            pltpu.VMEM((2, 4, 128, 192), BF16),
            pltpu.VMEM((2, 192, 512), BF16),
            pltpu.VMEM((2, 4, 8, 128), F32),
            pltpu.VMEM((4, 128, 128), F32),
            pltpu.SemaphoreType.DMA((40,)),
            pltpu.SemaphoreType.DMA((40,)),
            pltpu.SemaphoreType.DMA((6, 5, 3)),
            pltpu.SemaphoreType.DMA((6, 5, 3)),
            pltpu.SemaphoreType.DMA((3,)),
        ],
        compiler_params=pltpu.CompilerParams(
            collective_id=0, has_side_effects=True, vmem_limit_bytes=40 << 20
        ),
    )(x, w, top)


def body(inputs, weights, cotangent):
    rows = preconditioned(inputs.reshape(128, 512), weights[0, 0], cotangent.reshape(128, 512))
    return rows[None, None]


def solution(mesh):
    placed = (P(None, "dp", None), P("section", None, None, None), P(None, "dp", None))
    return jax.shard_map(
        body, mesh=mesh, in_specs=placed, out_specs=P("section", None, "dp", None), check_vma=False
    )
```

```python
import functools
import jax
import jax.numpy as jnp
from jax import lax
from jax.experimental import pallas as pl
from jax.experimental.pallas import tpu as pltpu
from jax.sharding import PartitionSpec as P

MESH = pl.DeviceIdType.MESH
HIGHEST = lax.Precision.HIGHEST
F32, BF16 = jnp.float32, jnp.bfloat16
gelu_coef = 0.7978845608
cubic_coef = 0.044715
damping_level = 0.1
loss_scale = 0.0078125

STRIDE = {"y": 16, "x": 4, "z": 1}
PAIRS = [(i, j) for i in range(4) for j in range(i, 4)]
ACT_GROUPS = [(0, 5, "xyz"), (5, 5, "yxz")]
GRAD_GROUPS = [(10, 5, "xyz"), (15, 5, "yxz")]
WEIGHT_GROUPS = [(20, 8, "xyz"), (28, 8, "yxz")]
GATHER_AXES = ["yx", "xy"]


class Place:
    def __init__(self):
        self.section = lax.axis_index("section")
        self.dp = lax.axis_index("dp")
        self.core = lax.rem(self.section, 2)
        self.high = lax.div(self.section, 2)
        self.at = {a: lax.rem(lax.div(self.dp, s), 4) for a, s in STRIDE.items()}

    def along(self, axis, delta):
        there = lax.rem(self.at[axis] + delta, 4)
        return there, (self.section, self.dp + (there - self.at[axis]) * STRIDE[axis])

    def other_high(self, delta):
        return (lax.rem(self.high + delta, 4) * 2 + self.core, self.dp)

    def sibling(self):
        return (self.section + 1 - 2 * self.core, self.dp)


def enter(place):
    barrier = pltpu.get_barrier_semaphore()
    peers = [place.other_high(t) for t in (2, 1, 3)]
    peers += [place.along(a, t)[1] for a in "zyx" for t in (2, 1, 3)] + [place.sibling()]
    for peer in peers:
        pl.semaphore_signal(barrier, inc=1, device_id=peer, device_id_type=MESH)
    pl.semaphore_wait(barrier, len(peers))


def remote(src, dst, send, recv, peer):
    return pltpu.make_async_remote_copy(
        src_ref=src, dst_ref=dst, send_sem=send, recv_sem=recv, device_id=peer, device_id_type=MESH
    )


def times(index, size):
    return pl.multiple_of(index * size, size)


class Gather:
    def __init__(self, place, own, full, send, recv):
        self.place, self.own, self.full, self.send, self.recv = place, own, full, send, recv
        self.sent = []

    def rows(self, half, coarse):
        last, first = (self.place.at[a] for a in GATHER_AXES[half])
        if coarse:
            return pl.ds(times(last, 128), 128)
        return pl.ds(pl.multiple_of(last * 128 + first * 32, 32), 32)

    def go(self, index, src, dst, peer):
        copy = remote(src, dst, self.send.at[index], self.recv.at[index], peer)
        copy.start()
        self.sent.append(copy)
        return copy

    def run(self):
        place, mine = self.place, self.full.at[self.place.core]
        numbers = iter(range(64))
        arrivals = {}
        for slot, t in ((1, 1), (2, 3), (3, 2)):
            for half in range(2):
                part = (self.rows(half, False), pl.ds(half * 256, 256))
                arrivals.setdefault((slot // 3, half), []).append(self.go(
                    next(numbers), self.own.at[part], mine.at[(slot, *part)], place.other_high(4 - t)
                ))
        swaps = [self.go(next(numbers), self.own, mine.at[0], place.sibling())]
        slots = [pl.ds(1, 2), pl.ds(3, 1)]
        for phase in range(2):
            for chunk in range(2):
                for half in range(2):
                    for copy in arrivals[chunk, half]:
                        copy.wait_recv()
                    block = mine.at[slots[chunk], self.rows(half, phase == 1), pl.ds(half * 256, 256)]
                    axis = GATHER_AXES[half][1 - phase]
                    arrivals[chunk, half] = [
                        self.go(next(numbers), block, block, place.along(axis, d)[1]) for d in (1, 3, 2)
                    ]
                    if phase == 1:
                        swaps.append(self.go(next(numbers), block, block, place.sibling()))
        for chunk in range(2):
            for number, d in enumerate((1, 3, 2)):
                for half in range(2):
                    arrivals[chunk, half][number].wait_recv()
                    origin = lax.rem(place.at[GATHER_AXES[half][0]] + 4 - d, 4)
                    block = mine.at[slots[chunk], pl.ds(times(origin, 128), 128), pl.ds(half * 256, 256)]
                    swaps.append(self.go(next(numbers), block, block, place.sibling()))
        for copy in swaps:
            copy.wait_recv()

    def close(self):
        for copy in self.sent:
            copy.wait_send()


class Sum:
    def __init__(self, place, group, index, part, full, bufs, send, recv):
        self.place, self.index, self.part, self.full = place, index, part, full
        self.first, self.count, self.axes = group
        self.recv1, self.sum1, self.recv2, self.sum2, self.recv3 = bufs
        self.send, self.recv = send, recv
        self.peers = {a: [place.along(a, d) for d in range(1, 4)] for a in self.axes}

    def copies(self, phase):
        blocks, at = pl.ds(self.first, self.count), self.place.at
        a1, a2, a3 = self.axes
        fine = pl.ds(pl.multiple_of(at[a1] * 32 + at[a2] * 8, 8), 8)
        axis = (a1, a2, a3, a2, a1)[phase]
        made = []
        for d, (there, peer) in enumerate(self.peers[axis]):
            if phase == 0:
                src, dst = self.part.at[blocks, pl.ds(times(there, 32), 32)], self.recv1.at[d, blocks]
            elif phase == 1:
                src, dst = self.sum1.at[blocks, pl.ds(times(there, 8), 8)], self.recv2.at[d, blocks]
            elif phase == 2:
                src, dst = self.sum2.at[blocks], self.recv3.at[d, blocks]
            elif phase == 3:
                src = dst = self.full.at[blocks, fine]
            else:
                src = dst = self.full.at[blocks, pl.ds(times(at[a1], 32), 32)]
            made.append(remote(
                src, dst, self.send.at[self.index, phase, d], self.recv.at[self.index, phase, d], peer
            ))
        return made

    def step(self, phase):
        blocks, at = pl.ds(self.first, self.count), self.place.at
        a1, a2, _ = self.axes
        if phase > 0:
            for copy in self.copies(phase - 1):
                copy.wait_recv()
        if phase == 1:
            mine = self.part[blocks, pl.ds(times(at[a1], 32), 32)]
            self.sum1[blocks] = (mine + self.recv1[0, blocks]) + (self.recv1[1, blocks] + self.recv1[2, blocks])
        elif phase == 2:
            mine = self.sum1[blocks, pl.ds(times(at[a2], 8), 8)]
            self.sum2[blocks] = (mine + self.recv2[0, blocks]) + (self.recv2[1, blocks] + self.recv2[2, blocks])
        elif phase == 3:
            fine = pl.ds(pl.multiple_of(at[a1] * 32 + at[a2] * 8, 8), 8)
            self.full[blocks, fine] = (self.sum2[blocks] + self.recv3[0, blocks]) + (
                self.recv3[1, blocks] + self.recv3[2, blocks]
            )
        if phase < 5:
            for copy in self.copies(phase):
                copy.start()

    def close(self):
        for phase in range(5):
            for copy in self.copies(phase):
                copy.wait_send()


def transposed_dot(left, right):
    return lax.dot_general(left, right, (((0,), (0,)), ((), ())), preferred_element_type=F32)


def thirds(value):
    high = value.astype(BF16)
    rest = value - high.astype(F32)
    middle = rest.astype(BF16)
    return high, middle, (rest - middle.astype(F32)).astype(BF16)


def panel_inverse(panels, lane0, between):
    sub = lax.broadcasted_iota(jnp.int32, (8, 128), 0)
    lane = lax.broadcasted_iota(jnp.int32, (8, 128), 1)
    pick = [sub == k for k in range(8)]
    for j in range(4):
        first = lane0 + 8 * j
        own = (lane >= first) & (lane < first + 8)
        eye = (lane - first == sub).astype(F32)
        for rows in panels:
            r = rows[j]
            cols = [jnp.broadcast_to(r[0][:, first + k:first + k + 1], (8, 128)) for k in range(8)]
            r = [jnp.where(own, eye, r[0])] + r[1:]
            for k in range(0, 8, 2):
                c0, c1 = cols[k], cols[k + 1]
                p, o, u, w = c0[k:k + 1, :], c1[k:k + 1, :], c0[k + 1:k + 2, :], c1[k + 1:k + 2, :]
                inv = 1.0 / (p * w - o * u)
                c0 = jnp.where(pick[k], -1.0, jnp.where(pick[k + 1], 0.0, c0))
                c1 = jnp.where(pick[k], 0.0, jnp.where(pick[k + 1], -1.0, c1))
                f0 = (c0 * w - c1 * u) * inv + jnp.where(pick[k], 1.0, 0.0)
                f1 = (c1 * p - c0 * o) * inv + jnp.where(pick[k + 1], 1.0, 0.0)
                for n in range(k + 2, 8):
                    v = cols[n]
                    cols[n] = (v - f0 * v[k:k + 1, :]) - f1 * v[k + 1:k + 2, :]
                r = [(v - f0 * v[k:k + 1, :]) - f1 * v[k + 1:k + 2, :] for v in r]
            rows[j] = r
            for t in range(1, 4):
                i = (j + t) % 4
                c = rows[i][0]
                acc = [jnp.where(own, 0.0, c)] + rows[i][1:]
                for k in range(8):
                    wide = jnp.broadcast_to(c[:, first + k:first + k + 1], (8, 128))
                    acc = [v - wide * p[k:k + 1, :] for v, p in zip(acc, r)]
                rows[i] = acc
        between(j)
    return panels


def inverses(m, ahead, lefts, rights, beside, many=2):
    row = lax.broadcasted_iota(jnp.int32, (128, 128), 0)
    lane = lax.broadcasted_iota(jnp.int32, (128, 128), 1)
    short = lane[:32]

    def change(b, blocks, tile, q, left, right, live):
        lane0 = 32 * q
        mine = (lane >= lane0) & (lane < lane0 + 32) & live
        keep = mine & ((row < lane0) | (row >= lane0 + 32))
        for i in blocks:
            moved = jnp.dot(left[i], right, preferred_element_type=F32)
            for t in range(4):
                value = m[b, tile[i], tile[t]]
                if t == 0:
                    value = jnp.where(keep if i == 0 else mine, 0.0, value)
                m[b, tile[i], tile[t]] = value - moved[:, t * 128:(t + 1) * 128]

    def step(k, carry):
        beside(k)
        tile = [lax.rem(k + t, 4) for t in range(4)]
        before = [lax.rem(k + 3 + t, 4) for t in range(4)]
        waiting = [(before, 3, [lefts[b, i] for i in range(4)], rights[b], k > 0) for b in range(many)]
        old = [[ahead[b, t] for t in range(4)] for b in range(many)]
        for q in range(4):
            lane0 = 32 * q
            rows = pl.ds(lane0, 32)
            panels = panel_inverse([[[v[8 * i:8 * i + 8] for v in o] for i in range(4)] for o in old], lane0, lambda j: [change(b, [j], *waiting[b]) for b in range(many)])
            following = []
            for b in range(many):
                new = [jnp.concatenate([panels[b][i][t] for i in range(4)], axis=0) for t in range(4)]
                for t in range(4):
                    m[b, k, tile[t], rows, :] = new[t]
                left = [jnp.where(short < lane0, -old[b][0], jnp.where(short < lane0 + 32, 0.0, old[b][0]))]
                left += [old[b][t] * jnp.where(k + t >= 4, -1.0, 1.0) for t in range(1, 4)]
                rh, rm, rl = thirds(jnp.concatenate(new, axis=1))
                right = jnp.concatenate([rh, rm, rh, rl, rm, rh], axis=0)
                turned = []
                for i in range(4):
                    lh, lm, ll = thirds(left[i])
                    turned.append(jnp.concatenate([lh, lh, lm, lh, lm, ll], axis=0).T)
                waiting[b] = (tile, q, turned, right, True)
                if q < 3:
                    some, block, turn = pl.ds(lane0 + 32, 32), k, turned[0][lane0 + 32:lane0 + 64]
                else:
                    some, block, turn = pl.ds(0, 32), tile[1], turned[1][:32]
                moved = jnp.dot(turn, right, preferred_element_type=F32)
                mine = (short >= lane0) & (short < lane0 + 32)
                nxt = []
                for t in range(4):
                    value = m[b, block, tile[t], some, :]
                    if t == 0:
                        value = jnp.where(mine, 0.0, value)
                    nxt.append(value - moved[:, t * 128:(t + 1) * 128])
                following.append(nxt)
            old = following
        for b in range(many):
            for t in range(4):
                ahead[b, t] = old[b][(t + 1) % 4]
                lefts[b, t] = waiting[b][2][t]
            rights[b] = waiting[b][3]
        return carry

    for b in range(many):
        for t in range(4):
            ahead[b, t] = m[b, 0, t, 0:32, :]
            lefts[b, t] = jnp.zeros((128, 192), BF16)
        rights[b] = jnp.zeros((192, 512), BF16)
    lax.fori_loop(0, 4, step, 0)
    for b in range(many):
        change(b, range(4), [3, 0, 1, 2], 3, [lefts[b, i] for i in range(4)], rights[b], True)


def spread(full, first, m, b, scale, column):
    row = lax.broadcasted_iota(jnp.int32, (128, 128), 0)
    lane = lax.broadcasted_iota(jnp.int32, (128, 128), 1)
    down = []
    for i in range(4):
        block = full[first + PAIRS.index((i, i))]
        diagonal = jnp.where(row == lane, block + damping_level, 0.0)
        scale[b, i] = lax.rsqrt(jnp.broadcast_to(jnp.sum(diagonal, axis=0, keepdims=True), (8, 128)))
        down.append(lax.rsqrt(jnp.broadcast_to(jnp.sum(diagonal, axis=1, keepdims=True), (128, 128))))
        if column is not None:
            column[i] = down[i]
    for t, (i, j) in enumerate(PAIRS):
        block = full[first + t]
        if i == j:
            block = jnp.where(row == lane, block + damping_level, block)
        block = (block * down[i]) * scale[b, j, 0:1, :]
        m[b, i, j] = block
        if i != j:
            m[b, j, i] = block.T


def finish(m, full, scale, column, row, out_ref):
    rows = pl.ds(pl.multiple_of(lax.rem(row, 128), 8), 8)
    block = lax.div(row, 128)
    total = None
    for i in range(4):
        left = (m[0, block, i, rows, :] * column[block, rows, :]) * scale[0, i]
        wide = jnp.concatenate([full[20 + i * 4 + j] for j in range(4)], axis=1)
        part = jnp.dot(left, wide, precision=HIGHEST, preferred_element_type=F32)
        total = part if total is None else total + part
    out = None
    for i in range(4):
        wide = jnp.concatenate([m[1, i, j] for j in range(4)], axis=1)
        left = total[:, i * 128:(i + 1) * 128] * scale[1, i]
        part = jnp.dot(left, wide, precision=HIGHEST, preferred_element_type=F32)
        out = part if out is None else out + part
    for j in range(4):
        out_ref[:, j * 128:(j + 1) * 128] = out[:, j * 128:(j + 1) * 128] * scale[1, j]


def kernel(x_hbm, w_hbm, top_hbm, out_ref, weights, kept, slopes, grads, top, part, full,
           recv1, sum1, recv2, sum2, recv3, m, ahead, lefts, rights, scale, column,
           gather_send, gather_recv, sum_send, sum_recv, local):
    place = Place()
    loads = [
        pltpu.make_async_copy(w_hbm, weights.at[place.core, 0], local.at[0]),
        pltpu.make_async_copy(x_hbm, kept.at[0], local.at[1]),
        pltpu.make_async_copy(top_hbm, top, local.at[2]),
    ]
    for load in loads:
        load.start()
    enter(place)
    gather = Gather(place, w_hbm, weights, gather_send, gather_recv)
    gather.run()
    for load in loads:
        load.wait()

    def weight_of(layer):
        t = lax.rem(lax.div(layer, 2) - place.high + 4, 4)
        return weights.at[lax.rem(layer, 2), t + lax.div(t, 2) - 2 * lax.div(t, 3)]

    def forward(layer, carry):
        x = kept[layer]
        z = jnp.dot(x, weight_of(layer)[...], preferred_element_type=F32)
        squared = z * z
        tangent = jnp.tanh(gelu_coef * (z + cubic_coef * squared * z))
        slopes[layer] = 0.5 * (1.0 + tangent) + 0.5 * z * (1.0 - tangent * tangent) * gelu_coef * (
            1.0 + 3.0 * cubic_coef * squared
        )
        kept[layer + 1] = (x.astype(F32) + 0.5 * z * (1.0 + tangent)).astype(BF16)
        return carry

    lax.fori_loop(0, 8, forward, 0)

    bufs = (recv1, sum1, recv2, sum2, recv3)
    make = lambda groups, base: [
        Sum(place, g, base + n, part, full, bufs, sum_send, sum_recv) for n, g in enumerate(groups)
    ]
    acts, gradsums, weightsums = make(ACT_GROUPS, 0), make(GRAD_GROUPS, 2), make(WEIGHT_GROUPS, 4)

    def step(groups, phase):
        for group in groups:
            group.step(phase)

    x = kept[place.section]
    for i in range(4):
        product = transposed_dot(x[:, i * 128:(i + 1) * 128], x[:, i * 128:]) * (1.0 / 8192.0)
        for j in range(i, 4):
            part[PAIRS.index((i, j))] = product[:, (j - i) * 128:(j - i + 1) * 128]
    step(acts, 0)

    def backward(number, upstream):
        layer = 7 - number
        grad = (upstream.astype(F32) * slopes[layer]).astype(BF16)
        grads[layer] = grad
        return (
            upstream.astype(F32)
            + lax.dot_general(grad, weight_of(layer)[...], (((1,), (1,)), ((), ())), preferred_element_type=F32)
        ).astype(BF16)

    upstream = (top[...].astype(F32) * loss_scale).astype(BF16)
    lax.fori_loop(0, 8, backward, upstream)
    g = grads[place.section]
    for i in range(4):
        product = transposed_dot(g[:, i * 128:(i + 1) * 128], g[:, i * 128:])
        for j in range(i, 4):
            part[10 + PAIRS.index((i, j))] = product[:, (j - i) * 128:(j - i + 1) * 128]
    step(gradsums, 0)
    step(acts, 1)
    for i in range(4):
        product = transposed_dot(x[:, i * 128:(i + 1) * 128], g)
        for j in range(4):
            part[20 + 4 * i + j] = product[:, j * 128:(j + 1) * 128]
    step(gradsums, 1)
    step(acts, 2)
    step(weightsums, 0)
    step(gradsums, 2)
    step(acts, 3)
    step(gradsums, 3)
    step(acts, 4)
    step(weightsums, 1)
    step(gradsums, 4)
    step(acts, 5)
    spread(full, 0, m, 0, scale, column)
    step(weightsums, 2)
    step(gradsums, 5)
    spread(full, 10, m, 1, scale, None)

    def beside(k):
        for number in range(1, 3):
            pl.when(k == number)(functools.partial(step, weightsums, number + 2))

    inverses(m, ahead, lefts, rights, beside)
    step(weightsums, 5)
    finish(m, full, scale, column, place.dp * 8, out_ref)
    gather.close()
    for group in acts + gradsums + weightsums:
        group.close()


def preconditioned(x, w, top):
    return pl.pallas_call(
        kernel,
        out_shape=jax.ShapeDtypeStruct((8, 512), F32),
        in_specs=[pl.BlockSpec(memory_space=pltpu.HBM)] * 3,
        out_specs=pl.BlockSpec(memory_space=pltpu.VMEM),
        scratch_shapes=[
            pltpu.VMEM((2, 4, 512, 512), BF16),
            pltpu.VMEM((9, 128, 512), BF16),
            pltpu.VMEM((8, 128, 512), F32),
            pltpu.VMEM((8, 128, 512), BF16),
            pltpu.VMEM((128, 512), BF16),
            pltpu.VMEM((36, 128, 128), F32),
            pltpu.VMEM((36, 128, 128), F32),
            pltpu.VMEM((3, 36, 32, 128), F32),
            pltpu.VMEM((36, 32, 128), F32),
            pltpu.VMEM((3, 36, 8, 128), F32),
            pltpu.VMEM((36, 8, 128), F32),
            pltpu.VMEM((3, 36, 8, 128), F32),
            pltpu.VMEM((2, 4, 4, 128, 128), F32),
            pltpu.VMEM((2, 4, 32, 128), F32),
            pltpu.VMEM((2, 4, 128, 192), BF16),
            pltpu.VMEM((2, 192, 512), BF16),
            pltpu.VMEM((2, 4, 8, 128), F32),
            pltpu.VMEM((4, 128, 128), F32),
            pltpu.SemaphoreType.DMA((64,)),
            pltpu.SemaphoreType.DMA((64,)),
            pltpu.SemaphoreType.DMA((6, 5, 3)),
            pltpu.SemaphoreType.DMA((6, 5, 3)),
            pltpu.SemaphoreType.DMA((3,)),
        ],
        compiler_params=pltpu.CompilerParams(
            collective_id=0, has_side_effects=True, vmem_limit_bytes=40 << 20
        ),
    )(x, w, top)


def body(inputs, weights, cotangent):
    rows = preconditioned(inputs.reshape(128, 512), weights[0, 0], cotangent.reshape(128, 512))
    return rows[None, None]


def solution(mesh):
    placed = (P(None, "dp", None), P("section", None, None, None), P(None, "dp", None))
    return jax.shard_map(
        body, mesh=mesh, in_specs=placed, out_specs=P("section", None, "dp", None), check_vma=False
    )
```

```python
import functools
import jax
import jax.numpy as jnp
from jax import lax
from jax.experimental import pallas as pl
from jax.experimental.pallas import tpu as pltpu
from jax.sharding import PartitionSpec as P

MESH = pl.DeviceIdType.MESH
HIGHEST = lax.Precision.HIGHEST
F32, BF16 = jnp.float32, jnp.bfloat16
gelu_coef = 0.7978845608
cubic_coef = 0.044715
damping_level = 0.1
loss_scale = 0.0078125

STRIDE = {"y": 16, "x": 4, "z": 1}
PAIRS = [(i, j) for i in range(4) for j in range(i, 4)]
ACT_GROUPS = [(0, 5, "xyz"), (5, 5, "yxz")]
GRAD_GROUPS = [(10, 5, "xyz"), (15, 5, "yxz")]
WEIGHT_GROUPS = [(20, 8, "xyz"), (28, 8, "yxz")]
GATHER_AXES = ["yx", "xy"]


class Place:
    def __init__(self):
        self.section = lax.axis_index("section")
        self.dp = lax.axis_index("dp")
        self.core = lax.rem(self.section, 2)
        self.high = lax.div(self.section, 2)
        self.at = {a: lax.rem(lax.div(self.dp, s), 4) for a, s in STRIDE.items()}

    def along(self, axis, delta):
        there = lax.rem(self.at[axis] + delta, 4)
        return there, (self.section, self.dp + (there - self.at[axis]) * STRIDE[axis])

    def other_high(self, delta):
        return (lax.rem(self.high + delta, 4) * 2 + self.core, self.dp)

    def sibling(self):
        return (self.section + 1 - 2 * self.core, self.dp)


def enter(place):
    barrier = pltpu.get_barrier_semaphore()
    peers = [place.other_high(t) for t in (2, 1, 3)]
    peers += [place.along(a, t)[1] for a in "zyx" for t in (2, 1, 3)] + [place.sibling()]
    for peer in peers:
        pl.semaphore_signal(barrier, inc=1, device_id=peer, device_id_type=MESH)
    pl.semaphore_wait(barrier, len(peers))


def remote(src, dst, send, recv, peer):
    return pltpu.make_async_remote_copy(
        src_ref=src, dst_ref=dst, send_sem=send, recv_sem=recv, device_id=peer, device_id_type=MESH
    )


def times(index, size):
    return pl.multiple_of(index * size, size)


class Gather:
    def __init__(self, place, own, full, send, recv):
        self.place, self.own, self.full, self.send, self.recv = place, own, full, send, recv
        self.sent = []

    def rows(self, half, coarse):
        last, first = (self.place.at[a] for a in GATHER_AXES[half])
        if coarse:
            return pl.ds(times(last, 128), 128)
        return pl.ds(pl.multiple_of(last * 128 + first * 32, 32), 32)

    def go(self, index, src, dst, peer):
        copy = remote(src, dst, self.send.at[index], self.recv.at[index], peer)
        copy.start()
        self.sent.append(copy)
        return copy

    def run(self, beside):
        place, mine = self.place, self.full.at[self.place.core]
        numbers = iter(range(64))
        arrivals = {}
        for slot, t in ((1, 1), (2, 3), (3, 2)):
            for half in range(2):
                part = (self.rows(half, False), pl.ds(half * 256, 256))
                arrivals.setdefault((slot // 3, half), []).append(self.go(
                    next(numbers), self.own.at[part], mine.at[(slot, *part)], place.other_high(4 - t)
                ))
        self.go(next(numbers), self.own, mine.at[0], place.sibling()).wait_recv()
        swaps = []
        beside(0)
        slots = [pl.ds(1, 2), pl.ds(3, 1)]
        for phase in range(2):
            for chunk in range(2):
                for half in range(2):
                    for copy in arrivals[chunk, half]:
                        copy.wait_recv()
                    block = mine.at[slots[chunk], self.rows(half, phase == 1), pl.ds(half * 256, 256)]
                    axis = GATHER_AXES[half][1 - phase]
                    arrivals[chunk, half] = [
                        self.go(next(numbers), block, block, place.along(axis, d)[1]) for d in (1, 3, 2)
                    ]
                    if phase == 1:
                        swaps.append(self.go(next(numbers), block, block, place.sibling()))
            beside(1 + phase)
        for chunk in range(2):
            for number, d in enumerate((1, 3, 2)):
                for half in range(2):
                    arrivals[chunk, half][number].wait_recv()
                    origin = lax.rem(place.at[GATHER_AXES[half][0]] + 4 - d, 4)
                    block = mine.at[slots[chunk], pl.ds(times(origin, 128), 128), pl.ds(half * 256, 256)]
                    swaps.append(self.go(next(numbers), block, block, place.sibling()))
        for copy in swaps:
            copy.wait_recv()

    def close(self):
        for copy in self.sent:
            copy.wait_send()


class Sum:
    def __init__(self, place, group, index, part, full, bufs, send, recv):
        self.place, self.index, self.part, self.full = place, index, part, full
        self.first, self.count, self.axes = group
        self.recv1, self.sum1, self.recv2, self.sum2, self.recv3 = bufs
        self.send, self.recv = send, recv
        self.peers = {a: [place.along(a, d) for d in range(1, 4)] for a in self.axes}

    def copies(self, phase):
        blocks, at = pl.ds(self.first, self.count), self.place.at
        a1, a2, a3 = self.axes
        fine = pl.ds(pl.multiple_of(at[a1] * 32 + at[a2] * 8, 8), 8)
        axis = (a1, a2, a3, a2, a1)[phase]
        made = []
        for d, (there, peer) in enumerate(self.peers[axis]):
            if phase == 0:
                src, dst = self.part.at[blocks, pl.ds(times(there, 32), 32)], self.recv1.at[d, blocks]
            elif phase == 1:
                src, dst = self.sum1.at[blocks, pl.ds(times(there, 8), 8)], self.recv2.at[d, blocks]
            elif phase == 2:
                src, dst = self.sum2.at[blocks], self.recv3.at[d, blocks]
            elif phase == 3:
                src = dst = self.full.at[blocks, fine]
            else:
                src = dst = self.full.at[blocks, pl.ds(times(at[a1], 32), 32)]
            made.append(remote(
                src, dst, self.send.at[self.index, phase, d], self.recv.at[self.index, phase, d], peer
            ))
        return made

    def step(self, phase):
        blocks, at = pl.ds(self.first, self.count), self.place.at
        a1, a2, _ = self.axes
        if phase > 0:
            for copy in self.copies(phase - 1):
                copy.wait_recv()
        if phase == 1:
            mine = self.part[blocks, pl.ds(times(at[a1], 32), 32)]
            self.sum1[blocks] = (mine + self.recv1[0, blocks]) + (self.recv1[1, blocks] + self.recv1[2, blocks])
        elif phase == 2:
            mine = self.sum1[blocks, pl.ds(times(at[a2], 8), 8)]
            self.sum2[blocks] = (mine + self.recv2[0, blocks]) + (self.recv2[1, blocks] + self.recv2[2, blocks])
        elif phase == 3:
            fine = pl.ds(pl.multiple_of(at[a1] * 32 + at[a2] * 8, 8), 8)
            self.full[blocks, fine] = (self.sum2[blocks] + self.recv3[0, blocks]) + (
                self.recv3[1, blocks] + self.recv3[2, blocks]
            )
        if phase < 5:
            for copy in self.copies(phase):
                copy.start()

    def close(self):
        for phase in range(5):
            for copy in self.copies(phase):
                copy.wait_send()


def transposed_dot(left, right):
    return lax.dot_general(left, right, (((0,), (0,)), ((), ())), preferred_element_type=F32)


def thirds(value):
    high = value.astype(BF16)
    rest = value - high.astype(F32)
    middle = rest.astype(BF16)
    return high, middle, (rest - middle.astype(F32)).astype(BF16)


def panel_inverse(panels, lane0, between):
    sub = lax.broadcasted_iota(jnp.int32, (8, 128), 0)
    lane = lax.broadcasted_iota(jnp.int32, (8, 128), 1)
    pick = [sub == k for k in range(8)]
    for j in range(4):
        first = lane0 + 8 * j
        own = (lane >= first) & (lane < first + 8)
        eye = (lane - first == sub).astype(F32)
        for rows in panels:
            r = rows[j]
            cols = [jnp.broadcast_to(r[0][:, first + k:first + k + 1], (8, 128)) for k in range(8)]
            r = [jnp.where(own, eye, r[0])] + r[1:]
            for k in range(0, 8, 2):
                c0, c1 = cols[k], cols[k + 1]
                p, o, u, w = c0[k:k + 1, :], c1[k:k + 1, :], c0[k + 1:k + 2, :], c1[k + 1:k + 2, :]
                inv = 1.0 / (p * w - o * u)
                c0 = jnp.where(pick[k], -1.0, jnp.where(pick[k + 1], 0.0, c0))
                c1 = jnp.where(pick[k], 0.0, jnp.where(pick[k + 1], -1.0, c1))
                f0 = (c0 * w - c1 * u) * inv + jnp.where(pick[k], 1.0, 0.0)
                f1 = (c1 * p - c0 * o) * inv + jnp.where(pick[k + 1], 1.0, 0.0)
                for n in range(k + 2, 8):
                    v = cols[n]
                    cols[n] = (v - f0 * v[k:k + 1, :]) - f1 * v[k + 1:k + 2, :]
                r = [(v - f0 * v[k:k + 1, :]) - f1 * v[k + 1:k + 2, :] for v in r]
            rows[j] = r
            for t in range(1, 4):
                i = (j + t) % 4
                c = rows[i][0]
                acc = [jnp.where(own, 0.0, c)] + rows[i][1:]
                for k in range(8):
                    wide = jnp.broadcast_to(c[:, first + k:first + k + 1], (8, 128))
                    acc = [v - wide * p[k:k + 1, :] for v, p in zip(acc, r)]
                rows[i] = acc
        between(j)
    return panels


def inverses(m, ahead, lefts, rights, beside, first, many):
    row = lax.broadcasted_iota(jnp.int32, (128, 128), 0)
    lane = lax.broadcasted_iota(jnp.int32, (128, 128), 1)
    short = lane[:32]

    def change(b, blocks, tile, q, left, right, live):
        lane0 = 32 * q
        mine = (lane >= lane0) & (lane < lane0 + 32) & live
        keep = mine & ((row < lane0) | (row >= lane0 + 32))
        for i in blocks:
            moved = jnp.dot(left[i], right, preferred_element_type=F32)
            for t in range(4):
                value = m[first + b, tile[i], tile[t]]
                if t == 0:
                    value = jnp.where(keep if i == 0 else mine, 0.0, value)
                m[first + b, tile[i], tile[t]] = value - moved[:, t * 128:(t + 1) * 128]

    def step(k, carry):
        beside(k)
        tile = [lax.rem(k + t, 4) for t in range(4)]
        before = [lax.rem(k + 3 + t, 4) for t in range(4)]
        waiting = [(before, 3, [lefts[first + b, i] for i in range(4)], rights[first + b], k > 0) for b in range(many)]
        old = [[ahead[first + b, t] for t in range(4)] for b in range(many)]
        for q in range(4):
            lane0 = 32 * q
            rows = pl.ds(lane0, 32)
            panels = panel_inverse([[[v[8 * i:8 * i + 8] for v in o] for i in range(4)] for o in old], lane0, lambda j: [change(b, [j], *waiting[b]) for b in range(many)])
            following = []
            for b in range(many):
                new = [jnp.concatenate([panels[b][i][t] for i in range(4)], axis=0) for t in range(4)]
                for t in range(4):
                    m[first + b, k, tile[t], rows, :] = new[t]
                left = [jnp.where(short < lane0, -old[b][0], jnp.where(short < lane0 + 32, 0.0, old[b][0]))]
                left += [old[b][t] * jnp.where(k + t >= 4, -1.0, 1.0) for t in range(1, 4)]
                rh, rm, rl = thirds(jnp.concatenate(new, axis=1))
                right = jnp.concatenate([rh, rm, rh, rl, rm, rh], axis=0)
                turned = []
                for i in range(4):
                    lh, lm, ll = thirds(left[i])
                    turned.append(jnp.concatenate([lh, lh, lm, lh, lm, ll], axis=0).T)
                waiting[b] = (tile, q, turned, right, True)
                if q < 3:
                    some, block, turn = pl.ds(lane0 + 32, 32), k, turned[0][lane0 + 32:lane0 + 64]
                else:
                    some, block, turn = pl.ds(0, 32), tile[1], turned[1][:32]
                moved = jnp.dot(turn, right, preferred_element_type=F32)
                mine = (short >= lane0) & (short < lane0 + 32)
                nxt = []
                for t in range(4):
                    value = m[first + b, block, tile[t], some, :]
                    if t == 0:
                        value = jnp.where(mine, 0.0, value)
                    nxt.append(value - moved[:, t * 128:(t + 1) * 128])
                following.append(nxt)
            old = following
        for b in range(many):
            for t in range(4):
                ahead[first + b, t] = old[b][(t + 1) % 4]
                lefts[first + b, t] = waiting[b][2][t]
            rights[first + b] = waiting[b][3]
        return carry

    for b in range(many):
        for t in range(4):
            ahead[first + b, t] = m[first + b, 0, t, 0:32, :]
            lefts[first + b, t] = jnp.zeros((128, 192), BF16)
        rights[first + b] = jnp.zeros((192, 512), BF16)
    lax.fori_loop(0, 4, step, 0)
    for b in range(many):
        change(b, range(4), [3, 0, 1, 2], 3, [lefts[first + b, i] for i in range(4)], rights[first + b], True)


def spread(full, first, m, b, scale, column):
    row = lax.broadcasted_iota(jnp.int32, (128, 128), 0)
    lane = lax.broadcasted_iota(jnp.int32, (128, 128), 1)
    down = []
    for i in range(4):
        block = full[first + PAIRS.index((i, i))]
        diagonal = jnp.where(row == lane, block + damping_level, 0.0)
        scale[b, i] = lax.rsqrt(jnp.broadcast_to(jnp.sum(diagonal, axis=0, keepdims=True), (8, 128)))
        down.append(lax.rsqrt(jnp.broadcast_to(jnp.sum(diagonal, axis=1, keepdims=True), (128, 128))))
        if column is not None:
            column[i] = down[i]
    for t, (i, j) in enumerate(PAIRS):
        block = full[first + t]
        if i == j:
            block = jnp.where(row == lane, block + damping_level, block)
        block = (block * down[i]) * scale[b, j, 0:1, :]
        m[b, i, j] = block
        if i != j:
            m[b, j, i] = block.T


def finish(m, full, scale, column, row, out_ref):
    rows = pl.ds(pl.multiple_of(lax.rem(row, 128), 8), 8)
    block = lax.div(row, 128)
    total = None
    for i in range(4):
        left = (m[0, block, i, rows, :] * column[block, rows, :]) * scale[0, i]
        wide = jnp.concatenate([full[20 + i * 4 + j] for j in range(4)], axis=1)
        part = jnp.dot(left, wide, precision=HIGHEST, preferred_element_type=F32)
        total = part if total is None else total + part
    out = None
    for i in range(4):
        wide = jnp.concatenate([m[1, i, j] for j in range(4)], axis=1)
        left = total[:, i * 128:(i + 1) * 128] * scale[1, i]
        part = jnp.dot(left, wide, precision=HIGHEST, preferred_element_type=F32)
        out = part if out is None else out + part
    for j in range(4):
        out_ref[:, j * 128:(j + 1) * 128] = out[:, j * 128:(j + 1) * 128] * scale[1, j]


def kernel(x_hbm, w_hbm, top_hbm, out_ref, weights, kept, slopes, grads, top, part, full,
           recv1, sum1, recv2, sum2, recv3, m, ahead, lefts, rights, scale, column,
           gather_send, gather_recv, sum_send, sum_recv, local):
    place = Place()
    loads = [
        pltpu.make_async_copy(w_hbm, weights.at[place.core, 0], local.at[0]),
        pltpu.make_async_copy(x_hbm, kept.at[0], local.at[1]),
        pltpu.make_async_copy(top_hbm, top, local.at[2]),
    ]
    for load in loads:
        load.start()
    enter(place)
    def weight_of(layer):
        t = lax.rem(lax.div(layer, 2) - place.high + 4, 4)
        return weights.at[lax.rem(layer, 2), t + lax.div(t, 2) - 2 * lax.div(t, 3)]

    def forward(layer, carry):
        x = kept[layer]
        z = jnp.dot(x, weight_of(layer)[...], preferred_element_type=F32)
        squared = z * z
        tangent = jnp.tanh(gelu_coef * (z + cubic_coef * squared * z))
        slopes[layer] = 0.5 * (1.0 + tangent) + 0.5 * z * (1.0 - tangent * tangent) * gelu_coef * (
            1.0 + 3.0 * cubic_coef * squared
        )
        kept[layer + 1] = (x.astype(F32) + 0.5 * z * (1.0 + tangent)).astype(BF16)
        return carry

    bufs = (recv1, sum1, recv2, sum2, recv3)
    make = lambda groups, base: [
        Sum(place, g, base + n, part, full, bufs, sum_send, sum_recv) for n, g in enumerate(groups)
    ]
    acts, gradsums, weightsums = make(ACT_GROUPS, 0), make(GRAD_GROUPS, 2), make(WEIGHT_GROUPS, 4)

    def step(groups, phase):
        for group in groups:
            group.step(phase)

    def act_sum():
        x = kept[place.section]
        for i in range(4):
            product = transposed_dot(x[:, i * 128:(i + 1) * 128], x[:, i * 128:]) * (1.0 / 8192.0)
            for j in range(i, 4):
                part[PAIRS.index((i, j))] = product[:, (j - i) * 128:(j - i + 1) * 128]
        step(acts, 0)

    early, late = pl.when(place.high == 0), pl.when(place.high != 0)

    def ahead_of_layers(number):
        if number == 0:
            forward(0, 0)
            act_sum()
        else:
            step(acts, number)

    gather = Gather(place, w_hbm, weights, gather_send, gather_recv)

    def beside_gather(number):
        if number == 0:
            for load in loads:
                load.wait()
        early(functools.partial(ahead_of_layers, number))

    gather.run(beside_gather)
    early(functools.partial(step, acts, 3))
    lax.fori_loop(0, 8, forward, 0)
    early(functools.partial(step, acts, 4))
    late(act_sum)

    def backward(number, upstream):
        layer = 7 - number
        grad = (upstream.astype(F32) * slopes[layer]).astype(BF16)
        grads[layer] = grad
        return (
            upstream.astype(F32)
            + lax.dot_general(grad, weight_of(layer)[...], (((1,), (1,)), ((), ())), preferred_element_type=F32)
        ).astype(BF16)

    upstream = (top[...].astype(F32) * loss_scale).astype(BF16)
    lax.fori_loop(0, 8, backward, upstream)
    g = grads[place.section]
    for i in range(4):
        product = transposed_dot(g[:, i * 128:(i + 1) * 128], g[:, i * 128:])
        for j in range(i, 4):
            part[10 + PAIRS.index((i, j))] = product[:, (j - i) * 128:(j - i + 1) * 128]
    step(gradsums, 0)
    late(functools.partial(step, acts, 1))
    x = kept[place.section]
    for i in range(4):
        product = transposed_dot(x[:, i * 128:(i + 1) * 128], g)
        for j in range(4):
            part[20 + 4 * i + j] = product[:, j * 128:(j + 1) * 128]

    def in_order(*steps):
        for groups, phase in steps:
            step(groups, phase)

    def at(table):
        def beside(k):
            for number, steps in table.items():
                pl.when(k == number)(functools.partial(in_order, *steps))
        return beside

    inverse_refs = (m, ahead, lefts, rights)
    last = at({1: [(weightsums, 3)], 2: [(weightsums, 4)]})

    def one_by_one():
        step(acts, 5)
        spread(full, 0, m, 0, scale, column)
        inverses(*inverse_refs, at({
            1: [(gradsums, 1), (weightsums, 0)], 2: [(gradsums, 2)], 3: [(gradsums, 3), (weightsums, 1)],
        }), 0, 1)
        in_order((gradsums, 4), (weightsums, 2), (gradsums, 5))
        spread(full, 10, m, 1, scale, None)
        inverses(*inverse_refs, last, 1, 1)

    def together():
        in_order((gradsums, 1), (acts, 2), (weightsums, 0), (gradsums, 2), (acts, 3), (gradsums, 3), (acts, 4),
                 (weightsums, 1), (gradsums, 4), (acts, 5))
        spread(full, 0, m, 0, scale, column)
        in_order((weightsums, 2), (gradsums, 5))
        spread(full, 10, m, 1, scale, None)
        inverses(*inverse_refs, last, 0, 2)

    early(one_by_one)
    late(together)
    step(weightsums, 5)
    finish(m, full, scale, column, place.dp * 8, out_ref)
    gather.close()
    for group in acts + gradsums + weightsums:
        group.close()


def preconditioned(x, w, top):
    return pl.pallas_call(
        kernel,
        out_shape=jax.ShapeDtypeStruct((8, 512), F32),
        in_specs=[pl.BlockSpec(memory_space=pltpu.HBM)] * 3,
        out_specs=pl.BlockSpec(memory_space=pltpu.VMEM),
        scratch_shapes=[
            pltpu.VMEM((2, 4, 512, 512), BF16),
            pltpu.VMEM((9, 128, 512), BF16),
            pltpu.VMEM((8, 128, 512), F32),
            pltpu.VMEM((8, 128, 512), BF16),
            pltpu.VMEM((128, 512), BF16),
            pltpu.VMEM((36, 128, 128), F32),
            pltpu.VMEM((36, 128, 128), F32),
            pltpu.VMEM((3, 36, 32, 128), F32),
            pltpu.VMEM((36, 32, 128), F32),
            pltpu.VMEM((3, 36, 8, 128), F32),
            pltpu.VMEM((36, 8, 128), F32),
            pltpu.VMEM((3, 36, 8, 128), F32),
            pltpu.VMEM((2, 4, 4, 128, 128), F32),
            pltpu.VMEM((2, 4, 32, 128), F32),
            pltpu.VMEM((2, 4, 128, 192), BF16),
            pltpu.VMEM((2, 192, 512), BF16),
            pltpu.VMEM((2, 4, 8, 128), F32),
            pltpu.VMEM((4, 128, 128), F32),
            pltpu.SemaphoreType.DMA((64,)),
            pltpu.SemaphoreType.DMA((64,)),
            pltpu.SemaphoreType.DMA((6, 5, 3)),
            pltpu.SemaphoreType.DMA((6, 5, 3)),
            pltpu.SemaphoreType.DMA((3,)),
        ],
        compiler_params=pltpu.CompilerParams(
            collective_id=0, has_side_effects=True, vmem_limit_bytes=40 << 20
        ),
    )(x, w, top)


def body(inputs, weights, cotangent):
    rows = preconditioned(inputs.reshape(128, 512), weights[0, 0], cotangent.reshape(128, 512))
    return rows[None, None]


def solution(mesh):
    placed = (P(None, "dp", None), P("section", None, None, None), P(None, "dp", None))
    return jax.shard_map(
        body, mesh=mesh, in_specs=placed, out_specs=P("section", None, "dp", None), check_vma=False
    )
```

```python
import functools
import jax
import jax.numpy as jnp
from jax import lax
from jax.experimental import pallas as pl
from jax.experimental.pallas import tpu as pltpu
from jax.sharding import PartitionSpec as P

MESH = pl.DeviceIdType.MESH
HIGHEST = lax.Precision.HIGHEST
F32, BF16 = jnp.float32, jnp.bfloat16
gelu_coef = 0.7978845608
cubic_coef = 0.044715
damping_level = 0.1
loss_scale = 0.0078125

STRIDE = {"y": 16, "x": 4, "z": 1}
PAIRS = [(i, j) for i in range(4) for j in range(i, 4)]
ACT_GROUPS = [(0, 5, "xyz"), (5, 5, "yxz")]
GRAD_GROUPS = [(10, 5, "xyz"), (15, 5, "yxz")]
WEIGHT_GROUPS = [(20, 8, "xyz"), (28, 8, "yxz")]
GATHER_AXES = ["yx", "xy"]


class Place:
    def __init__(self):
        self.section = lax.axis_index("section")
        self.dp = lax.axis_index("dp")
        self.core = lax.rem(self.section, 2)
        self.high = lax.div(self.section, 2)
        self.at = {a: lax.rem(lax.div(self.dp, s), 4) for a, s in STRIDE.items()}

    def along(self, axis, delta):
        there = lax.rem(self.at[axis] + delta, 4)
        return there, (self.section, self.dp + (there - self.at[axis]) * STRIDE[axis])

    def other_high(self, delta):
        return (lax.rem(self.high + delta, 4) * 2 + self.core, self.dp)

    def sibling(self):
        return (self.section + 1 - 2 * self.core, self.dp)


def enter(place):
    barrier = pltpu.get_barrier_semaphore()
    peers = [place.other_high(t) for t in (2, 1, 3)]
    peers += [place.along(a, t)[1] for a in "zyx" for t in (2, 1, 3)] + [place.sibling()]
    for peer in peers:
        pl.semaphore_signal(barrier, inc=1, device_id=peer, device_id_type=MESH)
    pl.semaphore_wait(barrier, len(peers))


def remote(src, dst, send, recv, peer):
    return pltpu.make_async_remote_copy(
        src_ref=src, dst_ref=dst, send_sem=send, recv_sem=recv, device_id=peer, device_id_type=MESH
    )


def times(index, size):
    return pl.multiple_of(index * size, size)


class Gather:
    def __init__(self, place, own, full, send, recv):
        self.place, self.own, self.full, self.send, self.recv = place, own, full, send, recv
        self.sent = []

    def rows(self, half, coarse):
        last, first = (self.place.at[a] for a in GATHER_AXES[half])
        if coarse:
            return pl.ds(times(last, 128), 128)
        return pl.ds(pl.multiple_of(last * 128 + first * 32, 32), 32)

    def go(self, index, src, dst, peer):
        copy = remote(src, dst, self.send.at[index], self.recv.at[index], peer)
        copy.start()
        self.sent.append(copy)
        return copy

    def run(self, beside):
        place, mine = self.place, self.full.at[self.place.core]
        numbers = iter(range(64))
        arrivals = {}
        for slot, t in ((1, 1), (2, 3), (3, 2)):
            for half in range(2):
                part = (self.rows(half, False), pl.ds(half * 256, 256))
                arrivals.setdefault((slot // 3, half), []).append(self.go(
                    next(numbers), self.own.at[part], mine.at[(slot, *part)], place.other_high(4 - t)
                ))
        self.go(next(numbers), self.own, mine.at[0], place.sibling()).wait_recv()
        swaps = []
        beside(0)
        slots = [pl.ds(1, 2), pl.ds(3, 1)]
        for phase in range(2):
            for chunk in range(2):
                for half in range(2):
                    for copy in arrivals[chunk, half]:
                        copy.wait_recv()
                    block = mine.at[slots[chunk], self.rows(half, phase == 1), pl.ds(half * 256, 256)]
                    axis = GATHER_AXES[half][1 - phase]
                    arrivals[chunk, half] = [
                        self.go(next(numbers), block, block, place.along(axis, d)[1]) for d in (1, 3, 2)
                    ]
                    if phase == 1:
                        swaps.append(self.go(next(numbers), block, block, place.sibling()))
            beside(1 + phase)
        for chunk in range(2):
            for number, d in enumerate((1, 3, 2)):
                for half in range(2):
                    arrivals[chunk, half][number].wait_recv()
                    origin = lax.rem(place.at[GATHER_AXES[half][0]] + 4 - d, 4)
                    block = mine.at[slots[chunk], pl.ds(times(origin, 128), 128), pl.ds(half * 256, 256)]
                    swaps.append(self.go(next(numbers), block, block, place.sibling()))
        for copy in swaps:
            copy.wait_recv()

    def close(self):
        for copy in self.sent:
            copy.wait_send()


class Sum:
    def __init__(self, place, group, index, part, full, bufs, send, recv):
        self.place, self.index, self.part, self.full = place, index, part, full
        self.first, self.count, self.axes = group
        self.recv1, self.sum1, self.recv2, self.sum2, self.recv3 = bufs
        self.send, self.recv = send, recv
        self.peers = {a: [place.along(a, d) for d in range(1, 4)] for a in self.axes}

    def copies(self, phase):
        blocks, at = pl.ds(self.first, self.count), self.place.at
        a1, a2, a3 = self.axes
        fine = pl.ds(pl.multiple_of(at[a1] * 32 + at[a2] * 8, 8), 8)
        axis = (a1, a2, a3, a2, a1)[phase]
        made = []
        for d, (there, peer) in enumerate(self.peers[axis]):
            if phase == 0:
                src, dst = self.part.at[blocks, pl.ds(times(there, 32), 32)], self.recv1.at[d, blocks]
            elif phase == 1:
                src, dst = self.sum1.at[blocks, pl.ds(times(there, 8), 8)], self.recv2.at[d, blocks]
            elif phase == 2:
                src, dst = self.sum2.at[blocks], self.recv3.at[d, blocks]
            elif phase == 3:
                src = dst = self.full.at[blocks, fine]
            else:
                src = dst = self.full.at[blocks, pl.ds(times(at[a1], 32), 32)]
            made.append(remote(
                src, dst, self.send.at[self.index, phase, d], self.recv.at[self.index, phase, d], peer
            ))
        return made

    def step(self, phase):
        blocks, at = pl.ds(self.first, self.count), self.place.at
        a1, a2, _ = self.axes
        if phase > 0:
            for copy in self.copies(phase - 1):
                copy.wait_recv()
        if phase == 1:
            mine = self.part[blocks, pl.ds(times(at[a1], 32), 32)]
            self.sum1[blocks] = (mine + self.recv1[0, blocks]) + (self.recv1[1, blocks] + self.recv1[2, blocks])
        elif phase == 2:
            mine = self.sum1[blocks, pl.ds(times(at[a2], 8), 8)]
            self.sum2[blocks] = (mine + self.recv2[0, blocks]) + (self.recv2[1, blocks] + self.recv2[2, blocks])
        elif phase == 3:
            fine = pl.ds(pl.multiple_of(at[a1] * 32 + at[a2] * 8, 8), 8)
            self.full[blocks, fine] = (self.sum2[blocks] + self.recv3[0, blocks]) + (
                self.recv3[1, blocks] + self.recv3[2, blocks]
            )
        if phase < 5:
            for copy in self.copies(phase):
                copy.start()

    def close(self, phases):
        for phase in phases:
            for copy in self.copies(phase):
                copy.wait_send()


def transposed_dot(left, right):
    return lax.dot_general(left, right, (((0,), (0,)), ((), ())), preferred_element_type=F32)


def thirds(value):
    high = value.astype(BF16)
    rest = value - high.astype(F32)
    middle = rest.astype(BF16)
    return high, middle, (rest - middle.astype(F32)).astype(BF16)


def panel_inverse(panels, lane0, between):
    sub = lax.broadcasted_iota(jnp.int32, (8, 128), 0)
    lane = lax.broadcasted_iota(jnp.int32, (8, 128), 1)
    pick = [sub == k for k in range(8)]
    for j in range(4):
        first = lane0 + 8 * j
        own = (lane >= first) & (lane < first + 8)
        eye = (lane - first == sub).astype(F32)
        for rows in panels:
            r = rows[j]
            cols = [jnp.broadcast_to(r[0][:, first + k:first + k + 1], (8, 128)) for k in range(8)]
            r = [jnp.where(own, eye, r[0])] + r[1:]
            for k in range(0, 8, 2):
                c0, c1 = cols[k], cols[k + 1]
                p, o, u, w = c0[k:k + 1, :], c1[k:k + 1, :], c0[k + 1:k + 2, :], c1[k + 1:k + 2, :]
                inv = 1.0 / (p * w - o * u)
                c0 = jnp.where(pick[k], -1.0, jnp.where(pick[k + 1], 0.0, c0))
                c1 = jnp.where(pick[k], 0.0, jnp.where(pick[k + 1], -1.0, c1))
                f0 = (c0 * w - c1 * u) * inv + jnp.where(pick[k], 1.0, 0.0)
                f1 = (c1 * p - c0 * o) * inv + jnp.where(pick[k + 1], 1.0, 0.0)
                for n in range(k + 2, 8):
                    v = cols[n]
                    cols[n] = (v - f0 * v[k:k + 1, :]) - f1 * v[k + 1:k + 2, :]
                r = [(v - f0 * v[k:k + 1, :]) - f1 * v[k + 1:k + 2, :] for v in r]
            rows[j] = r
            for t in range(1, 4):
                i = (j + t) % 4
                c = rows[i][0]
                acc = [jnp.where(own, 0.0, c)] + rows[i][1:]
                for k in range(8):
                    wide = jnp.broadcast_to(c[:, first + k:first + k + 1], (8, 128))
                    acc = [v - wide * p[k:k + 1, :] for v, p in zip(acc, r)]
                rows[i] = acc
        between(j)
    return panels


def inverses(m, ahead, lefts, rights, beside, first, many):
    row = lax.broadcasted_iota(jnp.int32, (128, 128), 0)
    lane = lax.broadcasted_iota(jnp.int32, (128, 128), 1)
    short = lane[:32]

    def change(b, blocks, tile, q, left, right, live):
        lane0 = 32 * q
        mine = (lane >= lane0) & (lane < lane0 + 32) & live
        keep = mine & ((row < lane0) | (row >= lane0 + 32))
        for i in blocks:
            moved = jnp.dot(left[i], right, preferred_element_type=F32)
            for t in range(4):
                value = m[first + b, tile[i], tile[t]]
                if t == 0:
                    value = jnp.where(keep if i == 0 else mine, 0.0, value)
                m[first + b, tile[i], tile[t]] = value - moved[:, t * 128:(t + 1) * 128]

    def step(k, carry):
        beside(k)
        tile = [lax.rem(k + t, 4) for t in range(4)]
        before = [lax.rem(k + 3 + t, 4) for t in range(4)]
        waiting = [(before, 3, [lefts[first + b, i] for i in range(4)], rights[first + b], k > 0) for b in range(many)]
        old = [[ahead[first + b, t] for t in range(4)] for b in range(many)]
        for q in range(4):
            lane0 = 32 * q
            rows = pl.ds(lane0, 32)
            panels = panel_inverse([[[v[8 * i:8 * i + 8] for v in o] for i in range(4)] for o in old], lane0, lambda j: [change(b, [j], *waiting[b]) for b in range(many)])
            following = []
            for b in range(many):
                new = [jnp.concatenate([panels[b][i][t] for i in range(4)], axis=0) for t in range(4)]
                for t in range(4):
                    m[first + b, k, tile[t], rows, :] = new[t]
                left = [jnp.where(short < lane0, -old[b][0], jnp.where(short < lane0 + 32, 0.0, old[b][0]))]
                left += [old[b][t] * jnp.where(k + t >= 4, -1.0, 1.0) for t in range(1, 4)]
                rh, rm, rl = thirds(jnp.concatenate(new, axis=1))
                right = jnp.concatenate([rh, rm, rh, rl, rm, rh], axis=0)
                turned = []
                for i in range(4):
                    lh, lm, ll = thirds(left[i])
                    turned.append(jnp.concatenate([lh, lh, lm, lh, lm, ll], axis=0).T)
                waiting[b] = (tile, q, turned, right, True)
                if q < 3:
                    some, block, turn = pl.ds(lane0 + 32, 32), k, turned[0][lane0 + 32:lane0 + 64]
                else:
                    some, block, turn = pl.ds(0, 32), tile[1], turned[1][:32]
                moved = jnp.dot(turn, right, preferred_element_type=F32)
                mine = (short >= lane0) & (short < lane0 + 32)
                nxt = []
                for t in range(4):
                    value = m[first + b, block, tile[t], some, :]
                    if t == 0:
                        value = jnp.where(mine, 0.0, value)
                    nxt.append(value - moved[:, t * 128:(t + 1) * 128])
                following.append(nxt)
            old = following
        for b in range(many):
            for t in range(4):
                ahead[first + b, t] = old[b][(t + 1) % 4]
                lefts[first + b, t] = waiting[b][2][t]
            rights[first + b] = waiting[b][3]
        return carry

    for b in range(many):
        for t in range(4):
            ahead[first + b, t] = m[first + b, 0, t, 0:32, :]
            lefts[first + b, t] = jnp.zeros((128, 192), BF16)
        rights[first + b] = jnp.zeros((192, 512), BF16)
    lax.fori_loop(0, 4, step, 0)
    for b in range(many):
        change(b, range(4), [3, 0, 1, 2], 3, [lefts[first + b, i] for i in range(4)], rights[first + b], True)


def spread(full, first, m, b, scale, column):
    row = lax.broadcasted_iota(jnp.int32, (128, 128), 0)
    lane = lax.broadcasted_iota(jnp.int32, (128, 128), 1)
    down = []
    for i in range(4):
        block = full[first + PAIRS.index((i, i))]
        diagonal = jnp.where(row == lane, block + damping_level, 0.0)
        scale[b, i] = lax.rsqrt(jnp.broadcast_to(jnp.sum(diagonal, axis=0, keepdims=True), (8, 128)))
        down.append(lax.rsqrt(jnp.broadcast_to(jnp.sum(diagonal, axis=1, keepdims=True), (128, 128))))
        if column is not None:
            column[i] = down[i]
    for t, (i, j) in enumerate(PAIRS):
        block = full[first + t]
        if i == j:
            block = jnp.where(row == lane, block + damping_level, block)
        block = (block * down[i]) * scale[b, j, 0:1, :]
        m[b, i, j] = block
        if i != j:
            m[b, j, i] = block.T


def finish(m, full, scale, column, row, out_ref):
    rows = pl.ds(pl.multiple_of(lax.rem(row, 128), 8), 8)
    block = lax.div(row, 128)
    total = None
    for i in range(4):
        left = (m[0, block, i, rows, :] * column[block, rows, :]) * scale[0, i]
        wide = jnp.concatenate([full[20 + i * 4 + j] for j in range(4)], axis=1)
        part = jnp.dot(left, wide, precision=HIGHEST, preferred_element_type=F32)
        total = part if total is None else total + part
    out = None
    for i in range(4):
        wide = jnp.concatenate([m[1, i, j] for j in range(4)], axis=1)
        left = total[:, i * 128:(i + 1) * 128] * scale[1, i]
        part = jnp.dot(left, wide, precision=HIGHEST, preferred_element_type=F32)
        out = part if out is None else out + part
    for j in range(4):
        out_ref[:, j * 128:(j + 1) * 128] = out[:, j * 128:(j + 1) * 128] * scale[1, j]


def kernel(x_hbm, w_hbm, top_hbm, out_ref, weights, kept, slopes, grads, top, part, full,
           recv1, sum1, recv2, sum2, recv3, m, ahead, lefts, rights, scale, column,
           gather_send, gather_recv, sum_send, sum_recv, local):
    place = Place()
    loads = [
        pltpu.make_async_copy(w_hbm, weights.at[place.core, 0], local.at[0]),
        pltpu.make_async_copy(x_hbm, kept.at[0], local.at[1]),
        pltpu.make_async_copy(top_hbm, top, local.at[2]),
    ]
    for load in loads:
        load.start()
    enter(place)
    def weight_of(layer):
        t = lax.rem(lax.div(layer, 2) - place.high + 4, 4)
        return weights.at[lax.rem(layer, 2), t + lax.div(t, 2) - 2 * lax.div(t, 3)]

    def forward(layer, carry):
        x = kept[layer]
        z = jnp.dot(x, weight_of(layer)[...], preferred_element_type=F32)
        squared = z * z
        tangent = jnp.tanh(gelu_coef * (z + cubic_coef * squared * z))
        slopes[layer] = 0.5 * (1.0 + tangent) + 0.5 * z * (1.0 - tangent * tangent) * gelu_coef * (
            1.0 + 3.0 * cubic_coef * squared
        )
        kept[layer + 1] = (x.astype(F32) + 0.5 * z * (1.0 + tangent)).astype(BF16)
        return carry

    bufs = (recv1, sum1, recv2, sum2, recv3)
    make = lambda groups, base: [
        Sum(place, g, base + n, part, full, bufs, sum_send, sum_recv) for n, g in enumerate(groups)
    ]
    acts, gradsums, weightsums = make(ACT_GROUPS, 0), make(GRAD_GROUPS, 2), make(WEIGHT_GROUPS, 4)

    def step(groups, phase):
        for group in groups:
            group.step(phase)

    def act_sum():
        x = kept[place.section]
        for i in range(4):
            product = transposed_dot(x[:, i * 128:(i + 1) * 128], x[:, i * 128:]) * (1.0 / 8192.0)
            for j in range(i, 4):
                part[PAIRS.index((i, j))] = product[:, (j - i) * 128:(j - i + 1) * 128]
        step(acts, 0)

    early, late = pl.when(place.high == 0), pl.when(place.high != 0)

    def ahead_of_layers(number):
        if number == 0:
            forward(0, 0)
            act_sum()
        else:
            step(acts, number)

    gather = Gather(place, w_hbm, weights, gather_send, gather_recv)

    def beside_gather(number):
        if number == 0:
            for load in loads:
                load.wait()
        early(functools.partial(ahead_of_layers, number))

    gather.run(beside_gather)
    early(functools.partial(step, acts, 3))
    lax.fori_loop(0, 8, forward, 0)
    early(functools.partial(step, acts, 4))
    late(act_sum)

    def backward(number, upstream):
        layer = 7 - number
        grad = (upstream.astype(F32) * slopes[layer]).astype(BF16)
        grads[layer] = grad
        return (
            upstream.astype(F32)
            + lax.dot_general(grad, weight_of(layer)[...], (((1,), (1,)), ((), ())), preferred_element_type=F32)
        ).astype(BF16)

    upstream = (top[...].astype(F32) * loss_scale).astype(BF16)
    lax.fori_loop(0, 8, backward, upstream)
    g = grads[place.section]
    for i in range(4):
        product = transposed_dot(g[:, i * 128:(i + 1) * 128], g[:, i * 128:])
        for j in range(i, 4):
            part[10 + PAIRS.index((i, j))] = product[:, (j - i) * 128:(j - i + 1) * 128]
    step(gradsums, 0)
    late(functools.partial(step, acts, 1))
    x = kept[place.section]
    for i in range(4):
        product = transposed_dot(x[:, i * 128:(i + 1) * 128], g)
        for j in range(4):
            part[20 + 4 * i + j] = product[:, j * 128:(j + 1) * 128]

    def in_order(*steps):
        for groups, phase in steps:
            step(groups, phase)

    def at(table):
        def beside(k):
            for number, steps in table.items():
                pl.when(k == number)(functools.partial(in_order, *steps))
        return beside

    inverse_refs = (m, ahead, lefts, rights)
    last = at({1: [(weightsums, 3)], 2: [(weightsums, 4)]})

    def close(groups, phases):
        for group in groups:
            group.close(phases)

    def close_some():
        close(acts, range(5))
        close(gradsums, range(4))
        close(weightsums, range(2))

    def one_by_one():
        step(acts, 5)
        spread(full, 0, m, 0, scale, column)
        inverses(*inverse_refs, at({
            1: [(gradsums, 1), (weightsums, 0)], 2: [(gradsums, 2)], 3: [(gradsums, 3), (weightsums, 1)],
        }), 0, 1)
        in_order((gradsums, 4), (weightsums, 2))
        close_some()
        step(gradsums, 5)
        spread(full, 10, m, 1, scale, None)
        inverses(*inverse_refs, last, 1, 1)

    def together():
        in_order((gradsums, 1), (acts, 2), (weightsums, 0), (gradsums, 2), (acts, 3), (gradsums, 3), (acts, 4),
                 (weightsums, 1), (gradsums, 4), (acts, 5))
        spread(full, 0, m, 0, scale, column)
        step(weightsums, 2)
        close_some()
        step(gradsums, 5)
        spread(full, 10, m, 1, scale, None)
        inverses(*inverse_refs, last, 0, 2)

    gather.close()
    early(one_by_one)
    late(together)
    step(weightsums, 5)
    finish(m, full, scale, column, place.dp * 8, out_ref)
    close(gradsums, range(4, 5))
    close(weightsums, range(2, 5))


def preconditioned(x, w, top):
    return pl.pallas_call(
        kernel,
        out_shape=jax.ShapeDtypeStruct((8, 512), F32),
        in_specs=[pl.BlockSpec(memory_space=pltpu.HBM)] * 3,
        out_specs=pl.BlockSpec(memory_space=pltpu.VMEM),
        scratch_shapes=[
            pltpu.VMEM((2, 4, 512, 512), BF16),
            pltpu.VMEM((9, 128, 512), BF16),
            pltpu.VMEM((8, 128, 512), F32),
            pltpu.VMEM((8, 128, 512), BF16),
            pltpu.VMEM((128, 512), BF16),
            pltpu.VMEM((36, 128, 128), F32),
            pltpu.VMEM((36, 128, 128), F32),
            pltpu.VMEM((3, 36, 32, 128), F32),
            pltpu.VMEM((36, 32, 128), F32),
            pltpu.VMEM((3, 36, 8, 128), F32),
            pltpu.VMEM((36, 8, 128), F32),
            pltpu.VMEM((3, 36, 8, 128), F32),
            pltpu.VMEM((2, 4, 4, 128, 128), F32),
            pltpu.VMEM((2, 4, 32, 128), F32),
            pltpu.VMEM((2, 4, 128, 192), BF16),
            pltpu.VMEM((2, 192, 512), BF16),
            pltpu.VMEM((2, 4, 8, 128), F32),
            pltpu.VMEM((4, 128, 128), F32),
            pltpu.SemaphoreType.DMA((64,)),
            pltpu.SemaphoreType.DMA((64,)),
            pltpu.SemaphoreType.DMA((6, 5, 3)),
            pltpu.SemaphoreType.DMA((6, 5, 3)),
            pltpu.SemaphoreType.DMA((3,)),
        ],
        compiler_params=pltpu.CompilerParams(
            collective_id=0, has_side_effects=True, vmem_limit_bytes=64 << 20
        ),
    )(x, w, top)


def body(inputs, weights, cotangent):
    rows = preconditioned(inputs.reshape(128, 512), weights[0, 0], cotangent.reshape(128, 512))
    return rows[None, None]


def solution(mesh):
    placed = (P(None, "dp", None), P("section", None, None, None), P(None, "dp", None))
    return jax.shard_map(
        body, mesh=mesh, in_specs=placed, out_specs=P("section", None, "dp", None), check_vma=False
    )
```

```python
import functools
import jax
import jax.numpy as jnp
from jax import lax
from jax.experimental import pallas as pl
from jax.experimental.pallas import tpu as pltpu
from jax.sharding import PartitionSpec as P

MESH = pl.DeviceIdType.MESH
HIGHEST = lax.Precision.HIGHEST
F32, BF16 = jnp.float32, jnp.bfloat16
gelu_coef = 0.7978845608
cubic_coef = 0.044715
damping_level = 0.1
loss_scale = 0.0078125

STRIDE = {"y": 16, "x": 4, "z": 1}
PAIRS = [(i, j) for i in range(4) for j in range(i, 4)]
ACT_GROUPS = [(0, 5, "xyz"), (5, 5, "yxz")]
GRAD_GROUPS = [(10, 5, "xyz"), (15, 5, "yxz")]
WEIGHT_GROUPS = [(20, 8, "xyz"), (28, 8, "yxz")]
GATHER_AXES = ["yx", "xy"]


class Place:
    def __init__(self):
        self.section = lax.axis_index("section")
        self.dp = lax.axis_index("dp")
        self.core = lax.rem(self.section, 2)
        self.high = lax.div(self.section, 2)
        self.at = {a: lax.rem(lax.div(self.dp, s), 4) for a, s in STRIDE.items()}

    def along(self, axis, delta):
        there = lax.rem(self.at[axis] + delta, 4)
        return there, (self.section, self.dp + (there - self.at[axis]) * STRIDE[axis])

    def other_high(self, delta):
        return (lax.rem(self.high + delta, 4) * 2 + self.core, self.dp)

    def sibling(self):
        return (self.section + 1 - 2 * self.core, self.dp)


def enter(place):
    barrier = pltpu.get_barrier_semaphore()
    peers = [place.other_high(t) for t in (2, 1, 3)]
    peers += [place.along(a, t)[1] for a in "zyx" for t in (2, 1, 3)] + [place.sibling()]
    for peer in peers:
        pl.semaphore_signal(barrier, inc=1, device_id=peer, device_id_type=MESH)
    pl.semaphore_wait(barrier, len(peers))


def remote(src, dst, send, recv, peer):
    return pltpu.make_async_remote_copy(
        src_ref=src, dst_ref=dst, send_sem=send, recv_sem=recv, device_id=peer, device_id_type=MESH
    )


def times(index, size):
    return pl.multiple_of(index * size, size)


class Gather:
    def __init__(self, place, own, full, send, recv):
        self.place, self.own, self.full, self.send, self.recv = place, own, full, send, recv
        self.sent = []

    def rows(self, half, coarse):
        last, first = (self.place.at[a] for a in GATHER_AXES[half])
        if coarse:
            return pl.ds(times(last, 128), 128)
        return pl.ds(pl.multiple_of(last * 128 + first * 32, 32), 32)

    def go(self, index, src, dst, peer):
        copy = remote(src, dst, self.send.at[index], self.recv.at[index], peer)
        copy.start()
        self.sent.append(copy)
        return copy

    def run(self, beside):
        place, mine = self.place, self.full.at[self.place.core]
        numbers = iter(range(64))
        arrivals = {}
        for slot, t in ((1, 1), (2, 3), (3, 2)):
            for half in range(2):
                part = (self.rows(half, False), pl.ds(half * 256, 256))
                arrivals.setdefault((slot // 3, half), []).append(self.go(
                    next(numbers), self.own.at[part], mine.at[(slot, *part)], place.other_high(4 - t)
                ))
        self.go(next(numbers), self.own, mine.at[0], place.sibling()).wait_recv()
        swaps = []
        beside(0)
        slots = [pl.ds(1, 2), pl.ds(3, 1)]
        for phase in range(2):
            for chunk in range(2):
                for half in range(2):
                    for copy in arrivals[chunk, half]:
                        copy.wait_recv()
                    block = mine.at[slots[chunk], self.rows(half, phase == 1), pl.ds(half * 256, 256)]
                    axis = GATHER_AXES[half][1 - phase]
                    arrivals[chunk, half] = [
                        self.go(next(numbers), block, block, place.along(axis, d)[1]) for d in (1, 3, 2)
                    ]
                    if phase == 1:
                        swaps.append(self.go(next(numbers), block, block, place.sibling()))
            beside(1 + phase)
        for chunk in range(2):
            for number, d in enumerate((1, 3, 2)):
                for half in range(2):
                    arrivals[chunk, half][number].wait_recv()
                    origin = lax.rem(place.at[GATHER_AXES[half][0]] + 4 - d, 4)
                    block = mine.at[slots[chunk], pl.ds(times(origin, 128), 128), pl.ds(half * 256, 256)]
                    swaps.append(self.go(next(numbers), block, block, place.sibling()))
        for copy in swaps:
            copy.wait_recv()

    def close(self):
        for copy in self.sent:
            copy.wait_send()


class Sum:
    def __init__(self, place, group, index, part, full, bufs, send, recv):
        self.place, self.index, self.part, self.full = place, index, part, full
        self.first, self.count, self.axes = group
        self.recv1, self.sum1, self.recv2, self.sum2, self.recv3 = bufs
        self.send, self.recv = send, recv
        self.peers = {a: [place.along(a, d) for d in range(1, 4)] for a in self.axes}

    def copies(self, phase):
        blocks, at = pl.ds(self.first, self.count), self.place.at
        a1, a2, a3 = self.axes
        fine = pl.ds(pl.multiple_of(at[a1] * 32 + at[a2] * 8, 8), 8)
        axis = (a1, a2, a3, a2, a1)[phase]
        made = []
        for d, (there, peer) in enumerate(self.peers[axis]):
            if phase == 0:
                src, dst = self.part.at[blocks, pl.ds(times(there, 32), 32)], self.recv1.at[d, blocks]
            elif phase == 1:
                src, dst = self.sum1.at[blocks, pl.ds(times(there, 8), 8)], self.recv2.at[d, blocks]
            elif phase == 2:
                src, dst = self.sum2.at[blocks], self.recv3.at[d, blocks]
            elif phase == 3:
                src = dst = self.full.at[blocks, fine]
            else:
                src = dst = self.full.at[blocks, pl.ds(times(at[a1], 32), 32)]
            made.append(remote(
                src, dst, self.send.at[self.index, phase, d], self.recv.at[self.index, phase, d], peer
            ))
        return made

    def step(self, phase):
        blocks, at = pl.ds(self.first, self.count), self.place.at
        a1, a2, _ = self.axes
        if phase > 0:
            for copy in self.copies(phase - 1):
                copy.wait_recv()
        if phase == 1:
            mine = self.part[blocks, pl.ds(times(at[a1], 32), 32)]
            self.sum1[blocks] = (mine + self.recv1[0, blocks]) + (self.recv1[1, blocks] + self.recv1[2, blocks])
        elif phase == 2:
            mine = self.sum1[blocks, pl.ds(times(at[a2], 8), 8)]
            self.sum2[blocks] = (mine + self.recv2[0, blocks]) + (self.recv2[1, blocks] + self.recv2[2, blocks])
        elif phase == 3:
            fine = pl.ds(pl.multiple_of(at[a1] * 32 + at[a2] * 8, 8), 8)
            self.full[blocks, fine] = (self.sum2[blocks] + self.recv3[0, blocks]) + (
                self.recv3[1, blocks] + self.recv3[2, blocks]
            )
        if phase < 5:
            for copy in self.copies(phase):
                copy.start()

    def close(self, phases):
        for phase in phases:
            for copy in self.copies(phase):
                copy.wait_send()


def transposed_dot(left, right):
    return lax.dot_general(left, right, (((0,), (0,)), ((), ())), preferred_element_type=F32)


def thirds(value):
    high = value.astype(BF16)
    rest = value - high.astype(F32)
    middle = rest.astype(BF16)
    return high, middle, (rest - middle.astype(F32)).astype(BF16)


def panel_inverse(panels, lane0, between):
    sub = lax.broadcasted_iota(jnp.int32, (8, 128), 0)
    lane = lax.broadcasted_iota(jnp.int32, (8, 128), 1)
    pick = [sub == k for k in range(8)]
    for j in range(4):
        first = lane0 + 8 * j
        own = (lane >= first) & (lane < first + 8)
        eye = (lane - first == sub).astype(F32)
        for rows in panels:
            r = rows[j]
            cols = [jnp.broadcast_to(r[0][:, first + k:first + k + 1], (8, 128)) for k in range(8)]
            r = [jnp.where(own, eye, r[0])] + r[1:]
            for k in range(0, 8, 2):
                c0, c1 = cols[k], cols[k + 1]
                p, o, u, w = c0[k:k + 1, :], c1[k:k + 1, :], c0[k + 1:k + 2, :], c1[k + 1:k + 2, :]
                inv = 1.0 / (p * w - o * u)
                c0 = jnp.where(pick[k], -1.0, jnp.where(pick[k + 1], 0.0, c0))
                c1 = jnp.where(pick[k], 0.0, jnp.where(pick[k + 1], -1.0, c1))
                f0 = (c0 * w - c1 * u) * inv + jnp.where(pick[k], 1.0, 0.0)
                f1 = (c1 * p - c0 * o) * inv + jnp.where(pick[k + 1], 1.0, 0.0)
                for n in range(k + 2, 8):
                    v = cols[n]
                    cols[n] = (v - f0 * v[k:k + 1, :]) - f1 * v[k + 1:k + 2, :]
                r = [(v - f0 * v[k:k + 1, :]) - f1 * v[k + 1:k + 2, :] for v in r]
            rows[j] = r
            for t in range(1, 4):
                i = (j + t) % 4
                c = rows[i][0]
                acc = [jnp.where(own, 0.0, c)] + rows[i][1:]
                for k in range(8):
                    wide = jnp.broadcast_to(c[:, first + k:first + k + 1], (8, 128))
                    acc = [v - wide * p[k:k + 1, :] for v, p in zip(acc, r)]
                rows[i] = acc
        between(j)
    return panels


def inverses(m, ahead, lefts, rights, beside, first, many):
    row = lax.broadcasted_iota(jnp.int32, (128, 128), 0)
    lane = lax.broadcasted_iota(jnp.int32, (128, 128), 1)
    short = lane[:32]

    def change(b, blocks, tile, q, left, right, live):
        lane0 = 32 * q
        mine = (lane >= lane0) & (lane < lane0 + 32) & live
        keep = mine & ((row < lane0) | (row >= lane0 + 32))
        for i in blocks:
            moved = jnp.dot(left[i], right, preferred_element_type=F32)
            for t in range(4):
                value = m[first + b, tile[i], tile[t]]
                if t == 0:
                    value = jnp.where(keep if i == 0 else mine, 0.0, value)
                m[first + b, tile[i], tile[t]] = value - moved[:, t * 128:(t + 1) * 128]

    def step(k, carry):
        beside(k)
        tile = [lax.rem(k + t, 4) for t in range(4)]
        before = [lax.rem(k + 3 + t, 4) for t in range(4)]
        waiting = [(before, 3, [lefts[first + b, i] for i in range(4)], rights[first + b], k > 0) for b in range(many)]
        old = [[ahead[first + b, t] for t in range(4)] for b in range(many)]
        for q in range(4):
            lane0 = 32 * q
            rows = pl.ds(lane0, 32)
            panels = panel_inverse([[[v[8 * i:8 * i + 8] for v in o] for i in range(4)] for o in old], lane0, lambda j: [change(b, [j], *waiting[b]) for b in range(many)])
            following = []
            for b in range(many):
                new = [jnp.concatenate([panels[b][i][t] for i in range(4)], axis=0) for t in range(4)]
                for t in range(4):
                    m[first + b, k, tile[t], rows, :] = new[t]
                left = [jnp.where(short < lane0, -old[b][0], jnp.where(short < lane0 + 32, 0.0, old[b][0]))]
                left += [old[b][t] * jnp.where(k + t >= 4, -1.0, 1.0) for t in range(1, 4)]
                rh, rm, rl = thirds(jnp.concatenate(new, axis=1))
                right = jnp.concatenate([rh, rm, rh, rl, rm, rh], axis=0)
                turned = []
                for i in range(4):
                    lh, lm, ll = thirds(left[i])
                    turned.append(jnp.concatenate([lh, lh, lm, lh, lm, ll], axis=0).T)
                waiting[b] = (tile, q, turned, right, True)
                if q < 3:
                    some, block, turn = pl.ds(lane0 + 32, 32), k, turned[0][lane0 + 32:lane0 + 64]
                else:
                    some, block, turn = pl.ds(0, 32), tile[1], turned[1][:32]
                moved = jnp.dot(turn, right, preferred_element_type=F32)
                mine = (short >= lane0) & (short < lane0 + 32)
                nxt = []
                for t in range(4):
                    value = m[first + b, block, tile[t], some, :]
                    if t == 0:
                        value = jnp.where(mine, 0.0, value)
                    nxt.append(value - moved[:, t * 128:(t + 1) * 128])
                following.append(nxt)
            old = following
        for b in range(many):
            for t in range(4):
                ahead[first + b, t] = old[b][(t + 1) % 4]
                lefts[first + b, t] = waiting[b][2][t]
            rights[first + b] = waiting[b][3]
        return carry

    for b in range(many):
        for t in range(4):
            ahead[first + b, t] = m[first + b, 0, t, 0:32, :]
            lefts[first + b, t] = jnp.zeros((128, 192), BF16)
        rights[first + b] = jnp.zeros((192, 512), BF16)
    lax.fori_loop(0, 4, step, 0)
    for b in range(many):
        change(b, range(4), [3, 0, 1, 2], 3, [lefts[first + b, i] for i in range(4)], rights[first + b], True)


def spread(full, first, m, b, scale, column):
    row = lax.broadcasted_iota(jnp.int32, (128, 128), 0)
    lane = lax.broadcasted_iota(jnp.int32, (128, 128), 1)
    down = []
    for i in range(4):
        block = full[first + PAIRS.index((i, i))]
        diagonal = jnp.where(row == lane, block + damping_level, 0.0)
        scale[b, i] = lax.rsqrt(jnp.broadcast_to(jnp.sum(diagonal, axis=0, keepdims=True), (8, 128)))
        down.append(lax.rsqrt(jnp.broadcast_to(jnp.sum(diagonal, axis=1, keepdims=True), (128, 128))))
        if column is not None:
            column[i] = down[i]
    for t, (i, j) in enumerate(PAIRS):
        block = full[first + t]
        if i == j:
            block = jnp.where(row == lane, block + damping_level, block)
        block = (block * down[i]) * scale[b, j, 0:1, :]
        m[b, i, j] = block
        if i != j:
            m[b, j, i] = block.T


def finish(m, full, scale, column, row, out_ref):
    rows = pl.ds(pl.multiple_of(lax.rem(row, 128), 8), 8)
    block = lax.div(row, 128)
    total = None
    for i in range(4):
        left = (m[0, block, i, rows, :] * column[block, rows, :]) * scale[0, i]
        wide = jnp.concatenate([full[20 + i * 4 + j] for j in range(4)], axis=1)
        part = jnp.dot(left, wide, precision=HIGHEST, preferred_element_type=F32)
        total = part if total is None else total + part
    out = None
    for i in range(4):
        wide = jnp.concatenate([m[1, i, j] for j in range(4)], axis=1)
        left = total[:, i * 128:(i + 1) * 128] * scale[1, i]
        part = jnp.dot(left, wide, precision=HIGHEST, preferred_element_type=F32)
        out = part if out is None else out + part
    for j in range(4):
        out_ref[:, j * 128:(j + 1) * 128] = out[:, j * 128:(j + 1) * 128] * scale[1, j]


def kernel(x_hbm, w_hbm, top_hbm, out_ref, weights, kept, slopes, grads, top, part, full,
           recv1, sum1, recv2, sum2, recv3, m, ahead, lefts, rights, scale, column,
           gather_send, gather_recv, sum_send, sum_recv, local):
    place = Place()
    loads = [
        pltpu.make_async_copy(w_hbm, weights.at[place.core, 0], local.at[0]),
        pltpu.make_async_copy(x_hbm, kept.at[0], local.at[1]),
        pltpu.make_async_copy(top_hbm, top, local.at[2]),
    ]
    for load in loads:
        load.start()
    enter(place)
    def weight_of(layer):
        t = lax.rem(lax.div(layer, 2) - place.high + 4, 4)
        return weights.at[lax.rem(layer, 2), t + lax.div(t, 2) - 2 * lax.div(t, 3)]

    def forward(layer, carry):
        x = kept[layer]
        z = jnp.dot(x, weight_of(layer)[...], preferred_element_type=F32)
        squared = z * z
        tangent = jnp.tanh(gelu_coef * (z + cubic_coef * squared * z))
        slopes[layer] = 0.5 * (1.0 + tangent) + 0.5 * z * (1.0 - tangent * tangent) * gelu_coef * (
            1.0 + 3.0 * cubic_coef * squared
        )
        kept[layer + 1] = (x.astype(F32) + 0.5 * z * (1.0 + tangent)).astype(BF16)
        return carry

    bufs = (recv1, sum1, recv2, sum2, recv3)
    make = lambda groups, base: [
        Sum(place, g, base + n, part, full, bufs, sum_send, sum_recv) for n, g in enumerate(groups)
    ]
    acts, gradsums, weightsums = make(ACT_GROUPS, 0), make(GRAD_GROUPS, 2), make(WEIGHT_GROUPS, 4)

    def step(groups, phase):
        for group in groups:
            group.step(phase)

    def act_sum():
        x = kept[place.section]
        for i in range(4):
            product = transposed_dot(x[:, i * 128:(i + 1) * 128], x[:, i * 128:]) * (1.0 / 8192.0)
            for j in range(i, 4):
                part[PAIRS.index((i, j))] = product[:, (j - i) * 128:(j - i + 1) * 128]
        step(acts, 0)

    early, late = pl.when(place.high == 0), pl.when(place.high != 0)

    def ahead_of_layers(number):
        if number == 0:
            forward(0, 0)
            act_sum()
        else:
            step(acts, number)

    gather = Gather(place, w_hbm, weights, gather_send, gather_recv)

    def beside_gather(number):
        if number == 0:
            for load in loads:
                load.wait()
        early(functools.partial(ahead_of_layers, number))

    gather.run(beside_gather)
    early(functools.partial(step, acts, 3))
    lax.fori_loop(0, 8, forward, 0, unroll=True)
    early(functools.partial(step, acts, 4))
    late(act_sum)

    def backward(number, upstream):
        layer = 7 - number
        grad = (upstream.astype(F32) * slopes[layer]).astype(BF16)
        grads[layer] = grad
        return (
            upstream.astype(F32)
            + lax.dot_general(grad, weight_of(layer)[...], (((1,), (1,)), ((), ())), preferred_element_type=F32)
        ).astype(BF16)

    upstream = (top[...].astype(F32) * loss_scale).astype(BF16)
    lax.fori_loop(0, 8, backward, upstream, unroll=True)
    g = grads[place.section]
    for i in range(4):
        product = transposed_dot(g[:, i * 128:(i + 1) * 128], g[:, i * 128:])
        for j in range(i, 4):
            part[10 + PAIRS.index((i, j))] = product[:, (j - i) * 128:(j - i + 1) * 128]
    step(gradsums, 0)
    late(functools.partial(step, acts, 1))
    x = kept[place.section]
    for i in range(4):
        product = transposed_dot(x[:, i * 128:(i + 1) * 128], g)
        for j in range(4):
            part[20 + 4 * i + j] = product[:, j * 128:(j + 1) * 128]

    def in_order(*steps):
        for groups, phase in steps:
            step(groups, phase)

    def at(table):
        def beside(k):
            for number, steps in table.items():
                pl.when(k == number)(functools.partial(in_order, *steps))
        return beside

    inverse_refs = (m, ahead, lefts, rights)
    last = at({1: [(weightsums, 3)], 2: [(weightsums, 4)]})

    def close(groups, phases):
        for group in groups:
            group.close(phases)

    def close_some():
        close(acts, range(5))
        close(gradsums, range(4))
        close(weightsums, range(2))

    def one_by_one():
        step(acts, 5)
        spread(full, 0, m, 0, scale, column)
        inverses(*inverse_refs, at({
            1: [(gradsums, 1), (weightsums, 0)], 2: [(gradsums, 2)], 3: [(gradsums, 3), (weightsums, 1)],
        }), 0, 1)
        in_order((gradsums, 4), (weightsums, 2))
        close_some()
        step(gradsums, 5)
        spread(full, 10, m, 1, scale, None)
        inverses(*inverse_refs, last, 1, 1)

    def together():
        in_order((gradsums, 1), (acts, 2), (weightsums, 0), (gradsums, 2), (acts, 3), (gradsums, 3), (acts, 4),
                 (weightsums, 1), (gradsums, 4), (acts, 5))
        spread(full, 0, m, 0, scale, column)
        step(weightsums, 2)
        close_some()
        step(gradsums, 5)
        spread(full, 10, m, 1, scale, None)
        inverses(*inverse_refs, last, 0, 2)

    gather.close()
    early(one_by_one)
    late(together)
    step(weightsums, 5)
    finish(m, full, scale, column, place.dp * 8, out_ref)
    close(gradsums, range(4, 5))
    close(weightsums, range(2, 5))


def preconditioned(x, w, top):
    return pl.pallas_call(
        kernel,
        out_shape=jax.ShapeDtypeStruct((8, 512), F32),
        in_specs=[pl.BlockSpec(memory_space=pltpu.HBM)] * 3,
        out_specs=pl.BlockSpec(memory_space=pltpu.VMEM),
        scratch_shapes=[
            pltpu.VMEM((2, 4, 512, 512), BF16),
            pltpu.VMEM((9, 128, 512), BF16),
            pltpu.VMEM((8, 128, 512), F32),
            pltpu.VMEM((8, 128, 512), BF16),
            pltpu.VMEM((128, 512), BF16),
            pltpu.VMEM((36, 128, 128), F32),
            pltpu.VMEM((36, 128, 128), F32),
            pltpu.VMEM((3, 36, 32, 128), F32),
            pltpu.VMEM((36, 32, 128), F32),
            pltpu.VMEM((3, 36, 8, 128), F32),
            pltpu.VMEM((36, 8, 128), F32),
            pltpu.VMEM((3, 36, 8, 128), F32),
            pltpu.VMEM((2, 4, 4, 128, 128), F32),
            pltpu.VMEM((2, 4, 32, 128), F32),
            pltpu.VMEM((2, 4, 128, 192), BF16),
            pltpu.VMEM((2, 192, 512), BF16),
            pltpu.VMEM((2, 4, 8, 128), F32),
            pltpu.VMEM((4, 128, 128), F32),
            pltpu.SemaphoreType.DMA((64,)),
            pltpu.SemaphoreType.DMA((64,)),
            pltpu.SemaphoreType.DMA((6, 5, 3)),
            pltpu.SemaphoreType.DMA((6, 5, 3)),
            pltpu.SemaphoreType.DMA((3,)),
        ],
        compiler_params=pltpu.CompilerParams(
            collective_id=0, has_side_effects=True, vmem_limit_bytes=64 << 20
        ),
    )(x, w, top)


def body(inputs, weights, cotangent):
    rows = preconditioned(inputs.reshape(128, 512), weights[0, 0], cotangent.reshape(128, 512))
    return rows[None, None]


def solution(mesh):
    placed = (P(None, "dp", None), P("section", None, None, None), P(None, "dp", None))
    return jax.shard_map(
        body, mesh=mesh, in_specs=placed, out_specs=P("section", None, "dp", None), check_vma=False
    )
```
